256 devices in a mesh: seq: 4 (over z_lo), hid: 64 (over z_hi, x, y, core).
Axes of the slice: x: 4, y: 4, z: 8 (z_hi: 2, z_lo: 4; z = z_hi * 4 + z_lo), core: 2. Of those that a mesh axis runs over, the one named last changes fastest.
Arguments:
- activations: bfloat16 [512, 8192], P(('seq', 'hid')), may hold values from -6 to 6
- ln_gain: float32 [8192], replicated, may hold values from 0.1 to 1.9
- in_blocks: bfloat16 [2304, 128, 128], P('hid'), may hold values from -0.1875 to 0.1875
- out_blocks: bfloat16 [2304, 128, 128], P('hid'), may hold values from -0.109375 to 0.109375
- block_row: int32 [2304], P('hid'), may hold values from 0 to 63, as said below
- block_col: int32 [2304], P('hid'), may hold values from 0 to 191, as said below
- block_count: int32 [64], P('hid'), may hold values from 12 to 36, as said below
- grad_out: bfloat16 [512, 8192], P(('seq', 'hid')), may hold values from -6 to 6
Outputs:
- layer_out: bfloat16 [512, 8192], P(('seq', 'hid'))
- grad_input: bfloat16 [512, 8192], P(('seq', 'hid'))
- grad_in_blocks: float32 [2304, 128, 128], P('hid')
- grad_out_blocks: float32 [2304, 128, 128], P('hid')
The draws below stay inside these ranges and needn't reach their ends.
Inputs may be any that keep to these rules, and one draw needn't show every extreme that they name: Slots j * 36 to (j + 1) * 36 - 1 belong to hid index j; within one hid index the slots name distinct pairs of block_row and block_col. `block_col`: slots of hid index j name block columns j * 3 to (j + 1) * 3 - 1. Slot s belongs to hid index j = s // 36 and is live when s - j * 36 < block_count[j]: the live slots of hid index j are its first block_count[j]; some hid index has all 36 live.
All inputs are finite; a program needn't handle non-finite values.
Results may differ from the reference program's by a relative error of at most 0.0053.
Values may be sent and summed in bfloat16 or wider, within the bound.
A program may use at most 128 MiB of HBM per device.

```python
import jax
import jax.numpy as jnp
from jax import lax

D = 8192
FF = 24576
BLOCK = 128
ROWS_ALL = 512
DB = 64
HCOL = 3
CAP = 36
SLOTS = 2304
N_HID = 64


def shared_positions(key):
    places = DB * HCOL
    keys = jax.random.split(key, N_HID)
    perms = jax.vmap(lambda k: jax.random.permutation(k, places))(keys)
    return perms[:, :CAP].astype(jnp.int32)


def draw_block_row(key, part):
    positions = shared_positions(key)
    return (positions // HCOL).reshape(N_HID * CAP).astype(jnp.int32)


def draw_block_col(key, part):
    positions = shared_positions(key)
    shard = jnp.arange(N_HID, dtype=jnp.int32)[:, None]
    return (shard * HCOL + positions % HCOL).reshape(N_HID * CAP).astype(jnp.int32)


def draw_block_count(key, part):
    key = jax.random.fold_in(key, 7)
    first, second, third = jax.random.split(key, 3)
    counts = jax.random.randint(first, (N_HID,), CAP // 3, CAP + 1).astype(jnp.int32)
    fullest = jax.random.randint(second, (), 0, N_HID).astype(jnp.int32)
    other = ((fullest + 1 + jax.random.randint(third, (), 0, N_HID - 1)) % N_HID).astype(jnp.int32)
    counts = counts.at[other].set(CAP // 3)
    counts = counts.at[fullest].set(CAP)
    return counts


def steps_of(stream_key, extent, cuts, low, high):
    level, own = 1.0, jax.random.fold_in(stream_key, 6)
    for position, shards_of in cuts:
        draws = jnp.exp(jax.random.uniform(jax.random.fold_in(own, position), (shards_of,), jnp.float32, low / len(cuts), high / len(cuts)))
        level = level * jnp.repeat(draws, extent[position] // shards_of).reshape([-1 if axis == position else 1 for axis in range(len(extent))])
    return level


def centred(rng, dims, deviation, bound, cuts=(), kind=jnp.bfloat16):
    drawn = jax.random.normal(rng, dims, jnp.float32) * deviation
    if len(cuts) > 0:
        drawn = steps_of(rng, dims, cuts, -0.22, 0.18) * drawn
    return jnp.clip(drawn, min=-bound, max=bound).astype(kind)


def setup_inputs(seed: int = 0) -> dict:
    arg_keys = jax.random.split(jax.random.key(seed), 9)
    return {
        "activations": centred(arg_keys[0], (ROWS_ALL, D), 1.0, 6.0, ((0, 256),)),
        "ln_gain": jnp.clip(1.0 + 0.18 * jax.random.normal(arg_keys[1], (D,), jnp.float32), 0.1, 1.9),
        "in_blocks": centred(arg_keys[2], (SLOTS, BLOCK, BLOCK), (D // 8) ** -0.5, 0.1875, ((0, 64),)),
        "out_blocks": centred(arg_keys[3], (SLOTS, BLOCK, BLOCK), (FF // 8) ** -0.5, 0.109375, ((0, 64),)),
        "block_row": draw_block_row(jax.random.fold_in(arg_keys[8], 71), 0),
        "block_col": draw_block_col(jax.random.fold_in(arg_keys[8], 71), 0),
        "block_count": draw_block_count(jax.random.fold_in(arg_keys[8], 71), 0),
        "grad_out": centred(arg_keys[7], (ROWS_ALL, D), 1.0, 6.0, ((0, 256),)),
    }


def normalize(activations, ln_gain):
    values = activations.astype(jnp.float32)
    row_mean = lax.optimization_barrier(jnp.mean(values, axis=-1, keepdims=True))
    centered = values - row_mean
    variance = lax.optimization_barrier(jnp.mean(centered * centered, axis=-1, keepdims=True))
    inv_std = lax.rsqrt(variance + 1e-05)
    x_hat = centered * inv_std
    return (x_hat, inv_std, (x_hat * ln_gain).astype(jnp.bfloat16))

def reference(activations, ln_gain, in_blocks, out_blocks, block_row, block_col, block_count, grad_out):
    high = lax.Precision.HIGHEST
    total_rows = activations.shape[0]
    local_cols = FF // BLOCK // N_HID
    row_blocks = D // BLOCK
    x_hat, inv_std, normed = normalize(activations, ln_gain)
    normed3 = normed.astype(jnp.float32).reshape(total_rows, row_blocks, BLOCK)
    grad3 = grad_out.astype(jnp.float32).reshape(total_rows, row_blocks, BLOCK)
    shard_ids = jnp.arange(N_HID, dtype=jnp.int32)
    rows2 = block_row.reshape(N_HID, CAP)
    cols2 = block_col.reshape(N_HID, CAP)
    inputs4 = in_blocks.reshape(N_HID, CAP, BLOCK, BLOCK)
    outputs4 = out_blocks.reshape(N_HID, CAP, BLOCK, BLOCK)

    def shard_step(carry, item):
        out_acc, normed_acc = carry
        shard, rows_here, cols_here, w_first, w_second, count = item
        live_mask = (jnp.arange(CAP, dtype=jnp.int32) < count).astype(jnp.float32)
        local = (cols_here - shard * local_cols).astype(jnp.int32)
        sel_row = jax.nn.one_hot(rows_here, row_blocks, dtype=jnp.float32) * live_mask[:, None]
        sel_col = jax.nn.one_hot(local, local_cols, dtype=jnp.float32) * live_mask[:, None]
        w_first = w_first.astype(jnp.float32)
        w_second = w_second.astype(jnp.float32)
        x_blocks = jnp.take(normed3, rows_here, axis=1)
        product = jnp.einsum('rsb,sbc->rsc', x_blocks, w_first, precision=high)
        pre = jnp.einsum('rsc,sh->rhc', product, sel_col, precision=high).reshape(total_rows, local_cols * BLOCK)
        hidden = jax.nn.silu(pre).astype(jnp.bfloat16)
        h_blocks = jnp.take(hidden.astype(jnp.float32).reshape(total_rows, local_cols, BLOCK), local, axis=1)
        y_prod = jnp.einsum('rsb,sbc->rsc', h_blocks, w_second, precision=high)
        out_acc = out_acc + jnp.einsum('rsc,sk->rkc', y_prod, sel_row, precision=high).reshape(total_rows, D)
        d_blocks = jnp.take(grad3, rows_here, axis=1)
        gh_prod = jnp.einsum('rsc,sbc->rsb', d_blocks, w_second, precision=high)
        grad_hidden = jnp.einsum('rsb,sh->rhb', gh_prod, sel_col, precision=high).reshape(total_rows, local_cols * BLOCK)
        sig = jax.nn.sigmoid(pre)
        grad_pre = (grad_hidden * sig * (1.0 + pre * (1.0 - sig))).astype(jnp.bfloat16)
        g_blocks = jnp.take(grad_pre.astype(jnp.float32).reshape(total_rows, local_cols, BLOCK), local, axis=1)
        gw_second = jnp.einsum('rsb,rsc->sbc', h_blocks, d_blocks, precision=high) * live_mask[:, None, None]
        gw_first = jnp.einsum('rsb,rsc->sbc', x_blocks, g_blocks, precision=high) * live_mask[:, None, None]
        gn_prod = jnp.einsum('rsc,sbc->rsb', g_blocks, w_first, precision=high)
        normed_acc = normed_acc + jnp.einsum('rsb,sk->rkb', gn_prod, sel_row, precision=high).reshape(total_rows, D)
        return ((out_acc, normed_acc), (gw_first, gw_second))
    start = (jnp.zeros((total_rows, D), jnp.float32), jnp.zeros((total_rows, D), jnp.float32))
    (out_sum, grad_normed), (gw_first, gw_second) = lax.scan(shard_step, start, (shard_ids, rows2, cols2, inputs4, outputs4, block_count))
    layer_out = (activations.astype(jnp.float32) + out_sum).astype(jnp.bfloat16)
    scaled = grad_normed * ln_gain
    mean_g = lax.optimization_barrier(jnp.mean(scaled, axis=-1, keepdims=True))
    mean_gx = lax.optimization_barrier(jnp.mean(scaled * x_hat, axis=-1, keepdims=True))
    grad_input = (inv_std * (scaled - mean_g - x_hat * mean_gx) + grad_out.astype(jnp.float32)).astype(jnp.bfloat16)
    return (layer_out, grad_input, gw_first.reshape(N_HID * CAP, BLOCK, BLOCK), gw_second.reshape(N_HID * CAP, BLOCK, BLOCK))
```

```python
import functools

import jax
import jax.numpy as jnp
from jax import lax
from jax.experimental import pallas as pl
from jax.experimental.pallas import tpu as pltpu
from jax.sharding import PartitionSpec as P

F32 = jnp.float32
BF16 = jnp.bfloat16
MESH = pl.DeviceIdType.MESH
WIDTH = 8192
SLOTS = 36
COLS = 3
CHUNK = 2
CHUNKS = 2 * SLOTS // CHUNK
LAG = 4


def place():
    seq, hid = lax.axis_index("seq"), lax.axis_index("hid")
    return seq, hid // 32, (hid // 8) % 4, (hid // 2) % 4, hid % 2


def device(seq, zh, x, y, core):
    return (seq, zh * 32 + x * 8 + y * 2 + core)


def remote(src, dst, send, recv, to):
    return pltpu.make_async_remote_copy(
        src_ref=src, dst_ref=dst, send_sem=send, recv_sem=recv, device_id=to, device_id_type=MESH
    )


def meet(peers):
    barrier = pltpu.get_barrier_semaphore()
    for peer in peers:
        pl.semaphore_signal(barrier, inc=1, device_id=peer, device_id_type=MESH)
    pl.semaphore_wait(barrier, len(peers))


def octet_peers(seq, zh, x, y, core):
    offsets = [(dx, dc) for dx in (2, 1, 3, 0) for dc in (0, 1) if (dx, dc) != (0, 0)]
    return [((x + dx) % 4, (core + dc) % 2) for dx, dc in offsets]


def layer_norm(act_ref):
    values = act_ref[...].astype(F32)
    mean = jnp.sum(values, axis=-1, keepdims=True) * (1.0 / WIDTH)
    centered = values - mean
    variance = jnp.sum(centered * centered, axis=-1, keepdims=True) * (1.0 / WIDTH)
    inv_std = lax.rsqrt(variance + 1e-05)
    return centered * inv_std, inv_std


def gather_kernel(
    act_ref, gain_ref, grad_ref, all_ref,
    wide, packed, landed,
    a2a_send, a2a_recv, zh_send, zh_recv, s1_send, s1_recv, s2_send, s2_recv, sw_send, sw_recv,
):
    seq, zh, x, y, core = place()
    me = x * 2 + core
    octet = octet_peers(seq, zh, x, y, core)
    xs = [(x + d) % 4 for d in (1, 2, 3)]
    ys = [(y + d) % 4 for d in (1, 2, 3)]
    partner = device(seq, 1 - zh, x, y, core)
    sibling = device(seq, zh, x, y, 1 - core)
    meet(
        [device(seq, zh, px, y, pc) for px, pc in octet]
        + [device(seq, zh, x, py, core) for py in ys]
        + [partner]
    )
    x_hat, _ = layer_norm(act_ref)
    for a, rows in enumerate((x_hat * gain_ref[...], grad_ref[...].astype(F32))):
        for p in range(64):
            wide[a, 2 * p : 2 * p + 2, :] = rows[:, p * 128 : (p + 1) * 128]
        packed[a] = wide[a].astype(BF16).reshape(8, 16, 128)
    copies = []
    for k, (px, pc) in enumerate(octet):
        copies.append(
            remote(
                packed.at[:, px * 2 + pc], landed.at[:, me], a2a_send.at[k], a2a_recv.at[k],
                device(seq, zh, px, y, pc),
            )
        )
        copies[-1].start()
    landed[:, me] = packed[:, me]
    for copy in copies:
        copy.wait_recv()
    for a in range(2):
        wide[a] = landed[a].astype(F32).reshape(128, 128)
        for p in range(8):
            first = wide[a, pl.ds(2 * p, 8, stride=16), :]
            second = wide[a, pl.ds(2 * p + 1, 8, stride=16), :]
            all_ref[a, x, core, p, zh, y] = jnp.concatenate([first, second], axis=0).astype(BF16)
    own = all_ref.at[:, x, core, :, zh, y]
    cross = remote(own, own, zh_send, zh_recv, partner)
    cross.start()

    def stage_one(plane, zp):
        out = []
        for d in range(3):
            block = all_ref.at[0, x, core, :, zp, y]
            out.append(
                remote(block, block, s1_send.at[plane, 0, d], s1_recv.at[plane, 0, d],
                       device(seq, zh, xs[d], y, core))
            )
            block = all_ref.at[1, x, core, :, zp, y]
            out.append(
                remote(block, block, s1_send.at[plane, 1, d], s1_recv.at[plane, 1, d],
                       device(seq, zh, x, ys[d], core))
            )
        for copy in out:
            copy.start()
        return out

    def stage_two(plane, zp):
        out = []
        for d in range(3):
            block = all_ref.at[0, :, core, :, zp, y]
            out.append(
                remote(block, block, s2_send.at[plane, 0, d], s2_recv.at[plane, 0, d],
                       device(seq, zh, x, ys[d], core))
            )
            block = all_ref.at[1, x, core, :, zp]
            out.append(
                remote(block, block, s2_send.at[plane, 1, d], s2_recv.at[plane, 1, d],
                       device(seq, zh, xs[d], y, core))
            )
        for copy in out:
            copy.start()
        return out

    def swap(plane, zp):
        out = []
        for a in range(2):
            block = all_ref.at[a, :, core, :, zp]
            out.append(remote(block, block, sw_send.at[plane, a], sw_recv.at[plane, a], sibling))
        for copy in out:
            copy.start()
        return out

    def landed_all(group):
        for copy in group:
            copy.wait_recv()

    one = stage_one(0, zh)
    landed_all(one)
    two = stage_two(0, zh)
    cross.wait_recv()
    one_far = stage_one(1, 1 - zh)
    landed_all(one_far)
    two_far = stage_two(1, 1 - zh)
    landed_all(two)
    sw = swap(0, zh)
    landed_all(two_far)
    sw_far = swap(1, 1 - zh)
    landed_all(sw)
    landed_all(sw_far)
    for copy in copies + [cross] + one + two + one_far + two_far + sw + sw_far:
        copy.wait_send()


def gather(act, gain, grad):
    vmem = pl.BlockSpec(memory_space=pltpu.VMEM)
    dma = pltpu.SemaphoreType.DMA
    return pl.pallas_call(
        gather_kernel,
        out_shape=jax.ShapeDtypeStruct((2, 4, 2, 8, 2, 4, 16, 128), BF16),
        in_specs=[vmem] * 3,
        out_specs=vmem,
        scratch_shapes=[
            pltpu.VMEM((2, 128, 128), F32),
            pltpu.VMEM((2, 8, 16, 128), BF16),
            pltpu.VMEM((2, 8, 16, 128), BF16),
            dma((7,)), dma((7,)), dma, dma,
            dma((2, 2, 3)), dma((2, 2, 3)), dma((2, 2, 3)), dma((2, 2, 3)),
            dma((2, 2)), dma((2, 2)),
        ],
        compiler_params=pltpu.CompilerParams(
            collective_id=1, has_side_effects=True, vmem_limit_bytes=32 << 20
        ),
        name="gather_rows",
    )(act, gain, grad)


def dot(a, b, dims):
    return lax.dot_general(a, b, (dims, ((), ())), preferred_element_type=F32)


GROUP = 4


def compute_kernel(
    row_ref, col_ref, count_ref, all_ref, in_ref, out_ref, sums_ref, grads_ref,
    pre, grad_hidden, hidden, grad_pre, total,
):
    first_col = lax.axis_index("hid") * COLS
    count = count_ref[0]
    pre[...] = jnp.zeros_like(pre)
    grad_hidden[...] = jnp.zeros_like(grad_hidden)

    def up(g, _):
        parts = []
        for k in range(GROUP):
            s = g * GROUP + k
            row = row_ref[s]
            live = s < count
            one = dot(all_ref[0, row], in_ref[s], ((1,), (0,)))
            two = dot(all_ref[1, row], out_ref[s], ((1,), (1,)))
            parts.append((s, jnp.where(live, one, 0.0), jnp.where(live, two, 0.0)))
        for s, one, two in parts:
            col = col_ref[s] - first_col
            pre[col] += one
            grad_hidden[col] += two
        return 0

    lax.fori_loop(0, SLOTS // GROUP, up, 0)
    for c in range(COLS):
        value = pre[c]
        sig = jax.nn.sigmoid(value)
        hidden[c] = (value * sig).astype(BF16)
        grad_pre[c] = (grad_hidden[c] * sig * (1.0 + value * (1.0 - sig))).astype(BF16)

    def clear(p, _):
        total[0, p] = jnp.zeros((128, 128), F32)
        total[1, p] = jnp.zeros((128, 128), F32)
        return 0

    lax.fori_loop(0, 64, clear, 0)

    def down(g, _):
        parts = []
        for k in range(GROUP):
            s = g * GROUP + k
            row = row_ref[s]
            col = col_ref[s] - first_col
            live = s < count
            h, gp = hidden[col], grad_pre[col]
            one = dot(h, out_ref[s], ((1,), (0,)))
            two = dot(gp, in_ref[s], ((1,), (1,)))
            three = dot(all_ref[0, row], gp, ((0,), (0,)))
            four = dot(h, all_ref[1, row], ((0,), (0,)))
            parts.append((s, row, jnp.where(live, one, 0.0), jnp.where(live, two, 0.0)))
            grads_ref[s] = jnp.where(live, three, 0.0).astype(BF16)
            grads_ref[s + SLOTS] = jnp.where(live, four, 0.0).astype(BF16)
        for s, row, one, two in parts:
            total[0, row] += one
            total[1, row] += two
        return 0

    lax.fori_loop(0, SLOTS // GROUP, down, 0)

    def narrow(p, _):
        sums_ref[0, p] = total[0, p].astype(BF16)
        sums_ref[1, p] = total[1, p].astype(BF16)
        return 0

    lax.fori_loop(0, 64, narrow, 0)


def compute(rows, cols, count, everything, in_blocks, out_blocks):
    vmem = pl.BlockSpec(memory_space=pltpu.VMEM)
    smem = pl.BlockSpec(memory_space=pltpu.SMEM)
    return pl.pallas_call(
        compute_kernel,
        out_shape=(
            jax.ShapeDtypeStruct((2, 64, 128, 128), BF16),
            jax.ShapeDtypeStruct((2 * SLOTS, 128, 128), BF16),
        ),
        in_specs=[smem] * 3 + [vmem] * 3,
        out_specs=(vmem, vmem),
        scratch_shapes=[
            pltpu.VMEM((COLS, 128, 128), F32),
            pltpu.VMEM((COLS, 128, 128), F32),
            pltpu.VMEM((COLS, 128, 128), BF16),
            pltpu.VMEM((COLS, 128, 128), BF16),
            pltpu.VMEM((2, 64, 128, 128), F32),
        ],
        compiler_params=pltpu.CompilerParams(vmem_limit_bytes=40 << 20),
        name="block_products",
    )(rows, cols, count, everything, in_blocks, out_blocks)


def reduce_kernel(
    act_ref, gain_ref, grad_ref, sums_ref, part_ref, out_ref, gin_ref, total_ref,
    swap_a, swap_b, half_a, half_b, near_a, near_b, quart_a, quart_b, far_a, far_b,
    keep, cross_src, cross_dst, wide, back, rows,
    end_in, mid_own, mid_in,
    sw_send, sw_recv, n_send, n_recv, f_send, f_recv, zh_send, zh_recv, b_send, b_recv,
    e_send, e_recv, m_send, m_recv, t_send, t_recv,
):
    seq, zh, x, y, core = place()
    me = x * 2 + core
    octet = octet_peers(seq, zh, x, y, core)
    partner = device(seq, 1 - zh, x, y, core)
    sibling = device(seq, zh, x, y, 1 - core)
    beside = device(seq + 1 - 2 * (seq % 2), zh, x, y, core)
    across = device(3 - seq, zh, x, y, core)
    is_mid = jnp.logical_or(seq == 1, seq == 2)
    is_end = jnp.logical_or(seq == 0, seq == 3)
    meet(
        [device(seq, zh, px, y, pc) for px, pc in octet]
        + [device(seq, zh, x, (y + d) % 4, core) for d in (1, 2, 3)]
        + [partner, beside, across]
    )

    def chunk(ref, k):
        return ref.at[pl.ds(k * CHUNK, CHUNK)]

    def end_copy(k):
        return remote(chunk(part_ref, k), chunk(end_in, k), e_send.at[k], e_recv.at[k], beside)

    def mid_copy(k):
        return remote(chunk(mid_own, k), chunk(mid_in, k), m_send.at[k], m_recv.at[k], across)

    def total_copy(k):
        return remote(chunk(total_ref, k), chunk(total_ref, k), t_send.at[k], t_recv.at[k], beside)

    def mid_first(k):
        end_copy(k).wait_recv()
        for j in range(CHUNK):
            s = k * CHUNK + j
            mid_own[s] = (end_in[s].astype(F32) + part_ref[s].astype(F32)).astype(BF16)
        mid_copy(k).start()

    def mid_second(k):
        mid_copy(k).wait_recv()
        for j in range(CHUNK):
            s = k * CHUNK + j
            total_ref[s] = (mid_own[s].astype(F32) + mid_in[s].astype(F32)).astype(BF16)
        total_copy(k).start()

    done = [0]

    def chain(steps):
        start, stop = done[0], min(done[0] + steps, CHUNKS + LAG)
        done[0] = stop

        @pl.when(is_mid)
        def _():
            def step(k, _):
                @pl.when(k < CHUNKS)
                def _():
                    mid_first(k)

                @pl.when(k >= LAG)
                def _():
                    mid_second(k - LAG)

                return 0

            lax.fori_loop(start, stop, step, 0)

    order = (2, 1, 3, 0)
    swaps = []
    for d in order:
        pair = (
            remote(sums_ref.at[0, (x + d) % 4, 1 - core], swap_a.at[d],
                   sw_send.at[0, d], sw_recv.at[0, d], sibling),
            remote(sums_ref.at[1, :, 1 - core, :, :, (y + d) % 4], swap_b.at[d],
                   sw_send.at[1, d], sw_recv.at[1, d], sibling),
        )
        for copy in pair:
            copy.start()
        swaps.append(pair)

    @pl.when(is_end)
    def _():
        def step(k, _):
            end_copy(k).start()
            return 0

        lax.fori_loop(0, CHUNKS, step, 0)

    nears = []
    for d, (copy_a, copy_b) in zip(order[:3], swaps):
        copy_a.wait_recv()

        def add_a(p, _):
            half_a[d, p] = (
                sums_ref[0, (x + d) % 4, core, p].astype(F32) + swap_a[d, p].astype(F32)
            ).astype(BF16)
            return 0

        lax.fori_loop(0, 8, add_a, 0)
        nears.append(
            remote(half_a.at[d], near_a.at[d], n_send.at[0, d], n_recv.at[0, d],
                   device(seq, zh, (x + d) % 4, y, core))
        )
        nears[-1].start()
        copy_b.wait_recv()

        def add_b(p, _):
            for v in range(4):
                half_b[d, v, p] = (
                    sums_ref[1, v, core, p, :, (y + d) % 4].astype(F32)
                    + swap_b[d, v, p].astype(F32)
                ).astype(BF16)
            return 0

        lax.fori_loop(0, 8, add_b, 0)
        nears.append(
            remote(half_b.at[d], near_b.at[d], n_send.at[1, d], n_recv.at[1, d],
                   device(seq, zh, x, (y + d) % 4, core))
        )
        nears[-1].start()
        chain(1)
    for copy in swaps[3]:
        copy.wait_recv()
    chain(6)
    for copy in nears:
        copy.wait_recv()

    def sum_a(p, _):
        value = sums_ref[0, x, core, p].astype(F32) + swap_a[0, p].astype(F32)
        for d in (1, 2, 3):
            value += near_a[d, p].astype(F32)
        quart_a[p] = value.astype(BF16)
        return 0

    lax.fori_loop(0, 8, sum_a, 0)
    fars = []
    for d in order[:3]:
        fars.append(
            remote(quart_a.at[:, :, (y + d) % 4], far_a.at[d], f_send.at[0, d], f_recv.at[0, d],
                   device(seq, zh, x, (y + d) % 4, core))
        )
        fars[-1].start()

    def sum_b(p, _):
        for v in range(4):
            value = sums_ref[1, v, core, p, :, y].astype(F32) + swap_b[0, v, p].astype(F32)
            for d in (1, 2, 3):
                value += near_b[d, v, p].astype(F32)
            quart_b[v, p] = value.astype(BF16)
        return 0

    lax.fori_loop(0, 8, sum_b, 0)
    for d in order[:3]:
        fars.append(
            remote(quart_b.at[(x + d) % 4], far_b.at[d], f_send.at[1, d], f_recv.at[1, d],
                   device(seq, zh, (x + d) % 4, y, core))
        )
        fars[-1].start()
    chain(3)
    for copy in fars:
        copy.wait_recv()

    def sum_far(p, _):
        one = quart_a[p, :, y].astype(F32)
        two = quart_b[x, p].astype(F32)
        for d in (1, 2, 3):
            one += far_a[d, p].astype(F32)
            two += far_b[d, p].astype(F32)
        keep[0, p] = one
        keep[1, p] = two
        cross_src[0, :, p] = one.astype(BF16)
        cross_src[1, :, p] = two.astype(BF16)
        return 0

    lax.fori_loop(0, 8, sum_far, 0)
    cross = remote(cross_src.at[:, 1 - zh], cross_dst, zh_send, zh_recv, partner)
    cross.start()
    chain(3)
    cross.wait_recv()
    for a in range(2):
        for p in range(8):
            value = keep[a, p, zh] + cross_dst[a, p].astype(F32)
            wide[a, pl.ds(2 * p, 8, stride=16), :] = value[0:8]
            wide[a, pl.ds(2 * p + 1, 8, stride=16), :] = value[8:16]
    for a in range(2):
        back[a] = wide[a].reshape(8, 16, 128)
    backs = []
    for k, (px, pc) in enumerate(octet):
        backs.append(
            remote(back.at[:, px * 2 + pc], rows.at[:, me], b_send.at[k], b_recv.at[k],
                   device(seq, zh, px, y, pc))
        )
        backs[-1].start()
    rows[:, me] = back[:, me]
    chain(2)
    for copy in backs:
        copy.wait_recv()
    sums = []
    for a in range(2):
        sums.append(
            jnp.concatenate(
                [rows[a, p // 8, 2 * (p % 8) : 2 * (p % 8) + 2, :] for p in range(64)], axis=1
            )
        )
    x_hat, inv_std = layer_norm(act_ref)
    out_ref[...] = (act_ref[...].astype(F32) + sums[0]).astype(BF16)
    scaled = sums[1] * gain_ref[...]
    mean_g = jnp.sum(scaled, axis=-1, keepdims=True) * (1.0 / WIDTH)
    mean_gx = jnp.sum(scaled * x_hat, axis=-1, keepdims=True) * (1.0 / WIDTH)
    gin_ref[...] = (
        inv_std * (scaled - mean_g - x_hat * mean_gx) + grad_ref[...].astype(F32)
    ).astype(BF16)
    chain(CHUNKS + LAG)

    @pl.when(is_mid)
    def _():
        def step(k, _):
            mid_copy(k).wait_send()
            total_copy(k).wait_send()
            return 0

        lax.fori_loop(0, CHUNKS, step, 0)

    @pl.when(is_end)
    def _():
        def step(k, _):
            end_copy(k).wait_send()
            total_copy(k).wait_recv()
            return 0

        lax.fori_loop(0, CHUNKS, step, 0)

    for pair in swaps:
        for copy in pair:
            copy.wait_send()
    for copy in nears + fars + [cross] + backs:
        copy.wait_send()


def reduce(act, gain, grad, sums, parts):
    vmem = pl.BlockSpec(memory_space=pltpu.VMEM)
    dma = pltpu.SemaphoreType.DMA
    slot = (2 * SLOTS, 128, 128)
    return pl.pallas_call(
        reduce_kernel,
        out_shape=(
            jax.ShapeDtypeStruct((2, WIDTH), BF16),
            jax.ShapeDtypeStruct((2, WIDTH), BF16),
            jax.ShapeDtypeStruct(slot, BF16),
        ),
        in_specs=[vmem] * 5,
        out_specs=(vmem, vmem, vmem),
        scratch_shapes=[
            pltpu.VMEM((4, 8, 2, 4, 16, 128), BF16),
            pltpu.VMEM((4, 4, 8, 2, 16, 128), BF16),
            pltpu.VMEM((4, 8, 2, 4, 16, 128), BF16),
            pltpu.VMEM((4, 4, 8, 2, 16, 128), BF16),
            pltpu.VMEM((4, 8, 2, 4, 16, 128), BF16),
            pltpu.VMEM((4, 4, 8, 2, 16, 128), BF16),
            pltpu.VMEM((8, 2, 4, 16, 128), BF16),
            pltpu.VMEM((4, 8, 2, 16, 128), BF16),
            pltpu.VMEM((4, 8, 2, 16, 128), BF16),
            pltpu.VMEM((4, 8, 2, 16, 128), BF16),
            pltpu.VMEM((2, 8, 2, 16, 128), F32),
            pltpu.VMEM((2, 2, 8, 16, 128), BF16),
            pltpu.VMEM((2, 8, 16, 128), BF16),
            pltpu.VMEM((2, 128, 128), F32),
            pltpu.VMEM((2, 8, 16, 128), F32),
            pltpu.VMEM((2, 8, 16, 128), F32),
            pltpu.VMEM(slot, BF16),
            pltpu.VMEM(slot, BF16),
            pltpu.VMEM(slot, BF16),
            dma((2, 4)), dma((2, 4)), dma((2, 4)), dma((2, 4)), dma((2, 4)), dma((2, 4)),
            dma, dma, dma((7,)), dma((7,)),
            dma((CHUNKS,)), dma((CHUNKS,)), dma((CHUNKS,)), dma((CHUNKS,)),
            dma((CHUNKS,)), dma((CHUNKS,)),
        ],
        compiler_params=pltpu.CompilerParams(
            collective_id=2, has_side_effects=True, vmem_limit_bytes=48 << 20
        ),
        name="reduce_sums",
    )(act, gain, grad, sums, parts)


def local(activations, ln_gain, in_blocks, out_blocks, block_row, block_col, block_count, grad_out):
    gain = ln_gain.reshape(1, WIDTH)
    everything = gather(activations, gain, grad_out)
    sums, parts = compute(
        block_row, block_col, block_count, everything.reshape(2, 64, 128, 128), in_blocks, out_blocks
    )
    layer_out, grad_input, totals = reduce(
        activations, gain, grad_out, sums.reshape(2, 4, 2, 8, 2, 4, 16, 128), parts
    )
    return (
        layer_out, grad_input, totals[:SLOTS].astype(F32), totals[SLOTS:].astype(F32),
    )


def solution(mesh):
    rows, blocks, slots = P(("seq", "hid"), None), P("hid", None, None), P("hid")
    in_specs = (rows, P(), blocks, blocks, slots, slots, slots, rows)
    out_specs = (rows, rows, blocks, blocks)
    return jax.shard_map(local, mesh=mesh, in_specs=in_specs, out_specs=out_specs, check_vma=False)
```

```python
import functools

import jax
import jax.numpy as jnp
from jax import lax
from jax.experimental import pallas as pl
from jax.experimental.pallas import tpu as pltpu
from jax.sharding import PartitionSpec as P

F32 = jnp.float32
BF16 = jnp.bfloat16
MESH = pl.DeviceIdType.MESH
WIDTH = 8192
SLOTS = 36
COLS = 3
CHUNK = 1
CHUNKS = SLOTS // CHUNK
LAG = 5


def place():
    seq, hid = lax.axis_index("seq"), lax.axis_index("hid")
    return seq, hid // 32, (hid // 8) % 4, (hid // 2) % 4, hid % 2


def device(seq, zh, x, y, core):
    return (seq, zh * 32 + x * 8 + y * 2 + core)


def remote(src, dst, send, recv, to):
    return pltpu.make_async_remote_copy(
        src_ref=src, dst_ref=dst, send_sem=send, recv_sem=recv, device_id=to, device_id_type=MESH
    )


def meet(peers):
    barrier = pltpu.get_barrier_semaphore()
    for peer in peers:
        pl.semaphore_signal(barrier, inc=1, device_id=peer, device_id_type=MESH)
    pl.semaphore_wait(barrier, len(peers))


def octet_peers(seq, zh, x, y, core):
    offsets = [(dx, dc) for dx in (2, 1, 3, 0) for dc in (0, 1) if (dx, dc) != (0, 0)]
    return [((x + dx) % 4, (core + dc) % 2) for dx, dc in offsets]


def layer_norm(act_ref):
    values = act_ref[...].astype(F32)
    mean = jnp.sum(values, axis=-1, keepdims=True) * (1.0 / WIDTH)
    centered = values - mean
    variance = jnp.sum(centered * centered, axis=-1, keepdims=True) * (1.0 / WIDTH)
    inv_std = lax.rsqrt(variance + 1e-05)
    return centered * inv_std, inv_std


def gather_kernel(
    act_hbm, gain_hbm, grad_hbm, all_ref, outer_y, outer_x,
    act_ref, gain_ref, grad_ref, wide, packed, landed,
    local_sem, a2a_send, a2a_recv, z_send, z_recv, s1_send, s1_recv,
    s2_send, s2_recv, fw_send, fw_recv, sw_send, sw_recv, o_send, o_recv,
):
    seq, zh, x, y, core = place()
    me = x * 2 + core
    octet = octet_peers(seq, zh, x, y, core)
    xs = [(x + d) % 4 for d in (1, 3, 2)]
    ys = [(y + d) % 4 for d in (1, 3, 2)]
    planes = (zh, 1 - zh)
    sibling = device(seq, zh, x, y, 1 - core)
    loads = [
        pltpu.make_async_copy(src, dst, local_sem.at[k])
        for k, (src, dst) in enumerate(
            ((act_hbm, act_ref), (gain_hbm, gain_ref), (grad_hbm, grad_ref))
        )
    ]
    for load in loads:
        load.start()
    targets = [(0, px, pc) for px, pc in octet] + [(1, px, pc) for px, pc in octet]
    targets.append((1, x, core))
    peers = [device(seq, planes[f], px, y, pc) for f, px, pc in targets]
    peers += [device(seq, zh, x, py, core) for py in ys]
    peers += [device((seq + d) % 4, zh, x, y, core) for d in (1, 2, 3)]
    barrier = pltpu.get_barrier_semaphore()
    for peer in peers:
        pl.semaphore_signal(barrier, inc=1, device_id=peer, device_id_type=MESH)
    for load in loads:
        load.wait()
    x_hat, _ = layer_norm(act_ref)
    for a, rows in enumerate((x_hat * gain_ref[...], grad_ref[...].astype(F32))):
        for p in range(64):
            wide[a, 2 * p : 2 * p + 2, :] = rows[:, p * 128 : (p + 1) * 128]
        packed[a] = wide[a].astype(BF16).reshape(8, 16, 128)
    pl.semaphore_wait(barrier, len(peers))
    near, far = [], []
    for k, (f, px, pc) in enumerate(targets):
        copy = remote(
            packed.at[:, px * 2 + pc], landed.at[zh, :, me], a2a_send.at[k], a2a_recv.at[k],
            peers[k],
        )
        copy.start()
        (far if f else near).append(copy)
    landed[zh, :, me] = packed[:, me]

    def relayout(zp):
        for a in range(2):
            wide[a] = landed[zp, a].astype(F32).reshape(128, 128)
            for p in range(8):
                first = wide[a, pl.ds(2 * p, 8, stride=16), :]
                second = wide[a, pl.ds(2 * p + 1, 8, stride=16), :]
                all_ref[a, x, core, p, zp, y] = jnp.concatenate([first, second], axis=0).astype(BF16)

    stage_ones, stage_twos, forwards, swaps, lines, outers = {}, {}, {}, [], [], []

    def stage_one(f):
        zp = planes[f]
        for a in (0, 1):
            block = all_ref.at[a, x, core, :, zp, y]
            out = []
            for d in range(3):
                to = device(seq, zh, xs[d], y, core) if a == 0 else device(seq, zh, x, ys[d], core)
                out.append(remote(block, block, s1_send.at[f, a, d], s1_recv.at[f, a, d], to))
                out[-1].start()
            stage_ones[f, a] = out

    def piece(f, other, nx, ny):
        return outer_x.at[other, nx] if f else outer_y.at[other, :, ny]

    def along_z(f):
        zp = planes[f]
        for d in (1, 2, 3):
            lines.append(
                remote(all_ref.at[1, x, core, :, zp, y], piece(f, seq, x, y),
                       z_send.at[f, d - 1], z_recv.at[f, d - 1],
                       device((seq + d) % 4, zh, x, y, core))
            )
            lines[-1].start()

    def outer_first():
        for f in range(2):
            for k in range(3):
                lines[3 * f + 2 - k].wait_recv()
                block = piece(f, (seq + k + 1) % 4, x, y)
                for d in range(3):
                    to = device(seq, zh, xs[d], y, core) if f else device(seq, zh, x, ys[d], core)
                    outers.append(
                        remote(block, block, o_send.at[f, k, d], o_recv.at[f, k, d], to)
                    )
                    outers[-1].start()

    def part(f, a, nx, ny, half):
        zp = planes[f]
        if a == 0:
            if half is None:
                return all_ref.at[0, :, core, :, zp, ny]
            return all_ref.at[0, pl.ds(2 * half, 2), core, :, zp, ny]
        if half is None:
            return all_ref.at[1, nx, core, :, zp]
        return all_ref.at[1, nx, core, pl.ds(4 * half, 4), zp]

    def ahead(a, d):
        if a == 0:
            return device(seq, zh, x, ys[d], core)
        return device(seq, zh, xs[d], y, core)

    def swap(f, a, k, block):
        copy = remote(block, block, sw_send.at[f, a, k], sw_recv.at[f, a, k], sibling)
        copy.start()
        swaps.append(copy)

    def stage_two(f):
        for a in (0, 1):
            for copy in stage_ones[f, a]:
                copy.wait_recv()
            block = part(f, a, x, y, None)
            out = []
            for d in range(2):
                out.append(
                    remote(block, block, s2_send.at[f, a, d], s2_recv.at[f, a, d], ahead(a, d))
                )
                out[-1].start()
            stage_twos[f, a] = out
        for a in (0, 1):
            swap(f, a, 0, part(f, a, x, y, None))

    def forward(f):
        for a in (0, 1):
            out = []
            for d in range(2):
                stage_twos[f, a][d].wait_recv()
                block = part(f, a, xs[1 - d], ys[1 - d], d)
                out.append(
                    remote(block, block, fw_send.at[f, a, d], fw_recv.at[f, a, d], ahead(a, d))
                )
                out[-1].start()
            forwards[f, a] = out
            for d in range(2):
                swap(f, a, 1 + d, part(f, a, xs[1 - d], ys[1 - d], None))

    def finish(f):
        for a in (0, 1):
            for copy in forwards[f, a]:
                copy.wait_recv()
            swap(f, a, 3, part(f, a, xs[2], ys[2], None))

    for copy in near:
        copy.wait_recv()
    relayout(zh)
    stage_one(0)
    for copy in far:
        copy.wait_recv()
    relayout(1 - zh)
    stage_one(1)
    stage_two(0)
    along_z(0)
    along_z(1)
    stage_two(1)
    forward(0)
    forward(1)
    outer_first()
    finish(0)
    finish(1)
    for copy in swaps + outers:
        copy.wait_recv()
    for copy in near + far + lines + swaps + outers:
        copy.wait_send()
    for group in (stage_ones, stage_twos, forwards):
        for copies in group.values():
            for copy in copies:
                copy.wait_send()


def gather(act, gain, grad):
    vmem = pl.BlockSpec(memory_space=pltpu.VMEM)
    hbm = pl.BlockSpec(memory_space=pltpu.HBM)
    dma = pltpu.SemaphoreType.DMA
    return pl.pallas_call(
        gather_kernel,
        out_shape=(
            jax.ShapeDtypeStruct((2, 4, 2, 8, 2, 4, 16, 128), BF16),
            jax.ShapeDtypeStruct((4, 8, 4, 16, 128), BF16),
            jax.ShapeDtypeStruct((4, 4, 8, 16, 128), BF16),
        ),
        in_specs=[hbm] * 3,
        out_specs=(vmem, vmem, vmem),
        scratch_shapes=[
            pltpu.VMEM((2, WIDTH), BF16),
            pltpu.VMEM((1, WIDTH), F32),
            pltpu.VMEM((2, WIDTH), BF16),
            pltpu.VMEM((2, 128, 128), F32),
            pltpu.VMEM((2, 8, 16, 128), BF16),
            pltpu.VMEM((2, 2, 8, 16, 128), BF16),
            dma((3,)), dma((15,)), dma((15,)), dma((2, 3)), dma((2, 3)),
            dma((2, 2, 3)), dma((2, 2, 3)), dma((2, 2, 2)), dma((2, 2, 2)),
            dma((2, 2, 2)), dma((2, 2, 2)), dma((2, 2, 4)), dma((2, 2, 4)),
            dma((2, 3, 3)), dma((2, 3, 3)),
        ],
        compiler_params=pltpu.CompilerParams(
            collective_id=1, has_side_effects=True, vmem_limit_bytes=12 << 20
        ),
        cost_estimate=pl.CostEstimate(flops=0, bytes_accessed=64 << 20, transcendentals=0),
        name="gather_rows",
    )(*(pltpu.with_memory_space_constraint(v, pltpu.HBM) for v in (act, gain, grad)))


def dot(a, b, dims):
    return lax.dot_general(a, b, (dims, ((), ())), preferred_element_type=F32)


GROUP = 4


def compute_kernel(
    row_hbm, col_hbm, count_ref, all_ref, in_hbm, out_hbm, sums_ref, grads_ref, hidden,
    row_ref, col_ref, in_ref, out_ref, pre, grad_hidden, grad_pre, total, local_sem,
):
    first_col = lax.axis_index("hid") * COLS
    loads = [
        pltpu.make_async_copy(src, dst, local_sem.at[k])
        for k, (src, dst) in enumerate(
            ((row_hbm, row_ref), (col_hbm, col_ref), (in_hbm, in_ref), (out_hbm, out_ref))
        )
    ]
    for load in loads:
        load.start()

    def clear(p, _):
        total[0, p] = jnp.zeros((128, 128), F32)
        total[1, p] = jnp.zeros((128, 128), F32)
        return 0

    lax.fori_loop(0, 64, clear, 0)
    pre[...] = jnp.zeros_like(pre)
    grad_hidden[...] = jnp.zeros_like(grad_hidden)
    for load in loads:
        load.wait()
    count = count_ref[0]

    def up(g, _):
        parts = []
        for k in range(GROUP):
            s = g * GROUP + k
            row = row_ref[s]
            live = s < count
            one = dot(all_ref[0, row], in_ref[s], ((1,), (0,)))
            two = dot(all_ref[1, row], out_ref[s], ((1,), (1,)))
            parts.append((s, jnp.where(live, one, 0.0), jnp.where(live, two, 0.0)))
        for s, one, two in parts:
            col = col_ref[s] - first_col
            pre[col] += one
            grad_hidden[col] += two
        return 0

    lax.fori_loop(0, SLOTS // GROUP, up, 0)
    for c in range(COLS):
        value = pre[c]
        sig = jax.nn.sigmoid(value)
        hidden[c] = (value * sig).astype(BF16)
        grad_pre[c] = (grad_hidden[c] * sig * (1.0 + value * (1.0 - sig))).astype(BF16)

    def down(g, _):
        parts = []
        for k in range(GROUP):
            s = g * GROUP + k
            row = row_ref[s]
            col = col_ref[s] - first_col
            live = s < count
            h, gp = hidden[col], grad_pre[col]
            one = dot(h, out_ref[s], ((1,), (0,)))
            two = dot(gp, in_ref[s], ((1,), (1,)))
            three = dot(all_ref[0, row], gp, ((0,), (0,)))
            parts.append((s, row, jnp.where(live, one, 0.0), jnp.where(live, two, 0.0)))
            grads_ref[s] = jnp.where(live, three, 0.0).astype(BF16)
        for s, row, one, two in parts:
            total[0, row] += one
            total[1, row] += two
        return 0

    lax.fori_loop(0, SLOTS // GROUP, down, 0)

    def narrow(p, _):
        sums_ref[0, p] = total[0, p].astype(BF16)
        sums_ref[1, p] = total[1, p].astype(BF16)
        return 0

    lax.fori_loop(0, 64, narrow, 0)


def compute(rows, cols, count, everything, in_blocks, out_blocks):
    vmem = pl.BlockSpec(memory_space=pltpu.VMEM)
    hbm = pl.BlockSpec(memory_space=pltpu.HBM)
    pin = functools.partial(pltpu.with_memory_space_constraint, memory_space=pltpu.HBM)
    return pl.pallas_call(
        compute_kernel,
        out_shape=(
            jax.ShapeDtypeStruct((2, 64, 128, 128), BF16),
            jax.ShapeDtypeStruct((SLOTS, 128, 128), BF16),
            jax.ShapeDtypeStruct((COLS, 128, 128), BF16),
        ),
        in_specs=[hbm] * 2 + [pl.BlockSpec(memory_space=pltpu.SMEM)] + [vmem] + [hbm] * 2,
        out_specs=(vmem, vmem, vmem),
        scratch_shapes=[
            pltpu.SMEM((SLOTS,), jnp.int32),
            pltpu.SMEM((SLOTS,), jnp.int32),
            pltpu.VMEM((SLOTS, 128, 128), BF16),
            pltpu.VMEM((SLOTS, 128, 128), BF16),
            pltpu.VMEM((COLS, 128, 128), F32),
            pltpu.VMEM((COLS, 128, 128), F32),
            pltpu.VMEM((COLS, 128, 128), BF16),
            pltpu.VMEM((2, 64, 128, 128), F32),
            pltpu.SemaphoreType.DMA((4,)),
        ],
        compiler_params=pltpu.CompilerParams(vmem_limit_bytes=24 << 20),
        name="block_products",
    )(pin(rows), pin(cols), count, everything, pin(in_blocks), pin(out_blocks))


def reduce_kernel(
    sums_ref, part_ref, hidden_ref, all_ref, outer_y, outer_x,
    rows, total_ref, hiddens_ref, grads_ref,
    swap_a, swap_b, half_a, half_b, near_a, near_b, quart_a, quart_b, far_a, far_b,
    wide, back,
    end_in, mid_own, mid_in,
    sw_send, sw_recv, n_send, n_recv, f_send, f_recv, b_send, b_recv,
    e_send, e_recv, m_send, m_recv, t_send, t_recv,
    h_send, h_recv, own_sem, ob_send, ob_recv, of_send, of_recv, os_send, os_recv,
):
    seq, zh, x, y, core = place()
    me = x * 2 + core
    octet = octet_peers(seq, zh, x, y, core)
    sibling = device(seq, zh, x, y, 1 - core)
    beside = device(seq + 1 - 2 * (seq % 2), zh, x, y, core)
    across = device(3 - seq, zh, x, y, core)
    is_mid = jnp.logical_or(seq == 1, seq == 2)
    is_end = jnp.logical_or(seq == 0, seq == 3)
    targets = [(zh, px, pc) for px, pc in octet] + [(1 - zh, px, pc) for px, pc in octet]
    targets.append((1 - zh, x, core))
    meet(
        [device(seq, zt, px, y, pc) for zt, px, pc in targets]
        + [device(seq, zh, x, (y + d) % 4, core) for d in (1, 2, 3)]
        + [device((seq + d) % 4, zh, x, y, core) for d in (1, 2, 3)]
    )
    others = [(seq + d) % 4 for d in (1, 2, 3)]
    xs = [(x + d) % 4 for d in (1, 3, 2)]
    ys = [(y + d) % 4 for d in (1, 3, 2)]

    def chunk(ref, k):
        return ref.at[pl.ds(k * CHUNK, CHUNK)]

    def end_copy(k):
        return remote(chunk(part_ref, k), chunk(end_in, k), e_send.at[k], e_recv.at[k], beside)

    def mid_copy(k):
        return remote(chunk(mid_own, k), chunk(mid_in, k), m_send.at[k], m_recv.at[k], across)

    def total_copy(k):
        return remote(chunk(total_ref, k), chunk(total_ref, k), t_send.at[k], t_recv.at[k], beside)

    def mid_first(k):
        end_copy(k).wait_recv()
        for j in range(CHUNK):
            s = k * CHUNK + j
            mid_own[s] = (end_in[s].astype(F32) + part_ref[s].astype(F32)).astype(BF16)
        mid_copy(k).start()

    def mid_second(k):
        mid_copy(k).wait_recv()
        for j in range(CHUNK):
            s = k * CHUNK + j
            total_ref[s] = (mid_own[s].astype(F32) + mid_in[s].astype(F32)).astype(BF16)
        total_copy(k).start()

    done = [0]

    def chain(steps):
        start, stop = done[0], min(done[0] + steps, CHUNKS + LAG)
        done[0] = stop

        @pl.when(is_mid)
        def _():
            def step(k, _):
                @pl.when(k < CHUNKS)
                def _():
                    mid_first(k)

                @pl.when(k >= LAG)
                def _():
                    mid_second(k - LAG)

                return 0

            lax.fori_loop(start, stop, step, 0)

    order = (2, 1, 3, 0)
    swaps = []
    for d in order:
        pair = (
            remote(sums_ref.at[0, (x + d) % 4, 1 - core], swap_a.at[d],
                   sw_send.at[0, d], sw_recv.at[0, d], sibling),
            remote(sums_ref.at[1, :, 1 - core, :, :, (y + d) % 4], swap_b.at[d],
                   sw_send.at[1, d], sw_recv.at[1, d], sibling),
        )
        for copy in pair:
            copy.start()
        swaps.append(pair)

    own_rows = pltpu.make_async_copy(all_ref.at[1], grads_ref.at[seq], own_sem)
    own_rows.start()
    hiddens_ref[seq] = hidden_ref[...]
    near_end = seq + 1 - 2 * (seq % 2)
    mid = 3 - seq
    far_end = mid + 1 - 2 * (mid % 2)

    def hidden_copy(source, k, to):
        block = hiddens_ref.at[source]
        return remote(block, block, h_send.at[k], h_recv.at[source], to)

    outer_b, outer_f, outer_s = [], [], []
    planes = (zh, 1 - zh)
    for other in others:
        for n in range(8):
            grads_ref[other, x, core, n, zh] = outer_y[other, n]
        for n in range(4):
            grads_ref[other, n, core, :, 1 - zh, y] = outer_x[other, n]

    def outer_block(other, f, nx, ny, half):
        if f:
            if half is None:
                return grads_ref.at[other, :, core, :, planes[1], ny]
            return grads_ref.at[other, pl.ds(2 * half, 2), core, :, planes[1], ny]
        if half is None:
            return grads_ref.at[other, nx, core, :, planes[0]]
        return grads_ref.at[other, nx, core, pl.ds(4 * half, 4), planes[0]]

    def outer_to(f, d):
        return device(seq, zh, x, ys[d], core) if f else device(seq, zh, xs[d], y, core)

    def outer_swap(k, f, n, block):
        copy = remote(block, block, os_send.at[k, f, n], os_recv.at[k, f, n], sibling)
        copy.start()
        outer_s.append(copy)

    def outer_second(k):
        other = others[k]
        for f in range(2):
            block = outer_block(other, f, x, y, None)
            for d in range(2):
                outer_b.append(
                    remote(block, block, ob_send.at[k, f, d], ob_recv.at[k, f, d], outer_to(f, d))
                )
                outer_b[-1].start()
        for f in range(2):
            outer_swap(k, f, 0, outer_block(other, f, x, y, None))

    def outer_forward(k):
        other = others[k]
        for f in range(2):
            for d in range(2):
                outer_b[4 * k + 2 * f + d].wait_recv()
                block = outer_block(other, f, xs[1 - d], ys[1 - d], d)
                outer_f.append(
                    remote(block, block, of_send.at[k, f, d], of_recv.at[k, f, d], outer_to(f, d))
                )
                outer_f[-1].start()
            for d in range(2):
                outer_swap(k, f, 1 + d, outer_block(other, f, xs[1 - d], ys[1 - d], None))

    def outer_finish(k):
        other = others[k]
        for f in range(2):
            for d in range(2):
                outer_f[4 * k + 2 * f + d].wait_recv()
            outer_swap(k, f, 3, outer_block(other, f, xs[2], ys[2], None))

    @pl.when(is_end)
    def _():
        def step(k, _):
            end_copy(k).start()
            return 0

        lax.fori_loop(0, 12, step, 0)
        hidden_copy(seq, 0, beside).start()
        lax.fori_loop(12, CHUNKS, step, 0)

    @pl.when(is_mid)
    def _():
        hidden_copy(seq, 0, beside).start()
        hidden_copy(seq, 1, across).start()

    outer_second(0)
    nears = []
    for d, (copy_a, copy_b) in zip(order[:3], swaps):
        copy_a.wait_recv()

        def add_a(p, _):
            half_a[d, p] = (
                sums_ref[0, (x + d) % 4, core, p].astype(F32) + swap_a[d, p].astype(F32)
            ).astype(BF16)
            return 0

        lax.fori_loop(0, 8, add_a, 0)
        nears.append(
            remote(half_a.at[d], near_a.at[d], n_send.at[0, d], n_recv.at[0, d],
                   device(seq, zh, (x + d) % 4, y, core))
        )
        nears[-1].start()
        copy_b.wait_recv()

        def add_b(p, _):
            for v in range(4):
                half_b[d, v, p] = (
                    sums_ref[1, v, core, p, :, (y + d) % 4].astype(F32)
                    + swap_b[d, v, p].astype(F32)
                ).astype(BF16)
            return 0

        lax.fori_loop(0, 8, add_b, 0)
        nears.append(
            remote(half_b.at[d], near_b.at[d], n_send.at[1, d], n_recv.at[1, d],
                   device(seq, zh, x, (y + d) % 4, core))
        )
        nears[-1].start()
        chain(2)
    for copy in swaps[3]:
        copy.wait_recv()
    for copy in nears:
        chain(3)
        copy.wait_recv()

    @pl.when(is_mid)
    def _():
        hidden_copy(near_end, 0, beside).wait_recv()
        hidden_copy(near_end, 2, across).start()
        hidden_copy(mid, 0, beside).wait_recv()
        hidden_copy(mid, 3, beside).start()


    def sum_a(p, _):
        value = sums_ref[0, x, core, p].astype(F32) + swap_a[0, p].astype(F32)
        for d in (1, 2, 3):
            value += near_a[d, p].astype(F32)
        quart_a[p] = value.astype(BF16)
        return 0

    lax.fori_loop(0, 8, sum_a, 0)
    fars = []
    for d in order[:3]:
        fars.append(
            remote(quart_a.at[:, :, (y + d) % 4], far_a.at[d], f_send.at[0, d], f_recv.at[0, d],
                   device(seq, zh, x, (y + d) % 4, core))
        )
        fars[-1].start()

    def sum_b(p, _):
        for v in range(4):
            value = sums_ref[1, v, core, p, :, y].astype(F32) + swap_b[0, v, p].astype(F32)
            for d in (1, 2, 3):
                value += near_b[d, v, p].astype(F32)
            quart_b[v, p] = value.astype(BF16)
        return 0

    lax.fori_loop(0, 8, sum_b, 0)
    for d in order[:3]:
        fars.append(
            remote(quart_b.at[(x + d) % 4], far_b.at[d], f_send.at[1, d], f_recv.at[1, d],
                   device(seq, zh, (x + d) % 4, y, core))
        )
        fars[-1].start()
    outer_second(1)
    outer_second(2)
    for copy in fars:
        chain(1)
        copy.wait_recv()

    def sum_far(p, _):
        one = quart_a[p, :, y].astype(F32)
        two = quart_b[x, p].astype(F32)
        for d in (1, 2, 3):
            one += far_a[d, p].astype(F32)
            two += far_b[d, p].astype(F32)
        for zt in range(2):
            for a, value in enumerate((one[zt], two[zt])):
                wide[zt, a, pl.ds(2 * p, 8, stride=16), :] = value[0:8]
                wide[zt, a, pl.ds(2 * p + 1, 8, stride=16), :] = value[8:16]
        return 0

    lax.fori_loop(0, 8, sum_far, 0)
    for zt in range(2):
        for a in range(2):
            back[zt, a] = wide[zt, a].astype(BF16).reshape(8, 16, 128)
    backs = []
    for k, (zt, px, pc) in enumerate(targets):
        backs.append(
            remote(back.at[zt, :, px * 2 + pc], rows.at[zh, :, me], b_send.at[k], b_recv.at[k],
                   device(seq, zt, px, y, pc))
        )
        backs[-1].start()
    rows[zh, :, me] = back[zh, :, me]
    outer_forward(0)
    chain(5)

    @pl.when(is_mid)
    def _():
        hidden_copy(far_end, 0, beside).wait_recv()
        hidden_copy(far_end, 4, beside).start()

    outer_forward(1)
    chain(2)
    for copy in backs:
        copy.wait_recv()
    outer_forward(2)
    chain(5)
    for k in range(3):
        chain(1)
        outer_finish(k)
    chain(CHUNKS + LAG)

    @pl.when(is_mid)
    def _():
        def step(k, _):
            mid_copy(k).wait_send()
            total_copy(k).wait_send()
            return 0

        lax.fori_loop(0, CHUNKS, step, 0)
        for k in range(5):
            hidden_copy(seq, k, beside).wait_send()

    @pl.when(is_end)
    def _():
        def step(k, _):
            end_copy(k).wait_send()
            total_copy(k).wait_recv()
            return 0

        lax.fori_loop(0, CHUNKS, step, 0)
        hidden_copy(seq, 0, beside).wait_send()
        for source in (near_end, mid, far_end):
            hidden_copy(source, 0, beside).wait_recv()

    for copy in outer_s:
        copy.wait_recv()
    own_rows.wait()
    for pair in swaps:
        for copy in pair:
            copy.wait_send()
    for copy in nears + fars + backs + outer_b + outer_f + outer_s:
        copy.wait_send()


def reduce(sums, parts, hidden, everything, outer_y, outer_x):
    vmem = pl.BlockSpec(memory_space=pltpu.VMEM)
    dma = pltpu.SemaphoreType.DMA
    slot = (SLOTS, 128, 128)
    return pl.pallas_call(
        reduce_kernel,
        out_shape=(
            jax.ShapeDtypeStruct((2, 2, 8, 16, 128), BF16),
            jax.ShapeDtypeStruct(slot, BF16),
            jax.ShapeDtypeStruct((4, COLS, 128, 128), BF16),
            jax.ShapeDtypeStruct((4, 4, 2, 8, 2, 4, 16, 128), BF16),
        ),
        in_specs=[vmem] * 6,
        out_specs=(vmem,) * 4,
        scratch_shapes=[
            pltpu.VMEM((4, 8, 2, 4, 16, 128), BF16),
            pltpu.VMEM((4, 4, 8, 2, 16, 128), BF16),
            pltpu.VMEM((4, 8, 2, 4, 16, 128), BF16),
            pltpu.VMEM((4, 4, 8, 2, 16, 128), BF16),
            pltpu.VMEM((4, 8, 2, 4, 16, 128), BF16),
            pltpu.VMEM((4, 4, 8, 2, 16, 128), BF16),
            pltpu.VMEM((8, 2, 4, 16, 128), BF16),
            pltpu.VMEM((4, 8, 2, 16, 128), BF16),
            pltpu.VMEM((4, 8, 2, 16, 128), BF16),
            pltpu.VMEM((4, 8, 2, 16, 128), BF16),
            pltpu.VMEM((2, 2, 128, 128), F32),
            pltpu.VMEM((2, 2, 8, 16, 128), BF16),
            pltpu.VMEM(slot, BF16),
            pltpu.VMEM(slot, BF16),
            pltpu.VMEM(slot, BF16),
            dma((2, 4)), dma((2, 4)), dma((2, 4)), dma((2, 4)), dma((2, 4)), dma((2, 4)),
            dma((15,)), dma((15,)),
            dma((CHUNKS,)), dma((CHUNKS,)), dma((CHUNKS,)), dma((CHUNKS,)),
            dma((CHUNKS,)), dma((CHUNKS,)),
            dma((5,)), dma((4,)), dma, dma((3, 2, 2)), dma((3, 2, 2)),
            dma((3, 2, 2)), dma((3, 2, 2)), dma((3, 2, 4)), dma((3, 2, 4)),
        ],
        compiler_params=pltpu.CompilerParams(
            collective_id=2, has_side_effects=True, vmem_limit_bytes=22 << 20
        ),
        cost_estimate=pl.CostEstimate(flops=0, bytes_accessed=64 << 20, transcendentals=0),
        name="reduce_sums",
    )(sums, parts, hidden, everything, outer_y, outer_x)


STEP = 6


def finish_kernel(
    row_hbm, col_hbm, count_ref, act_ref, gain_ref, grad_ref, sums_ref,
    hidden_ref, grads_ref, total_ref, layer_ref, gin_ref, in_ref, out_ref,
    turned, row_ref, col_ref, local_sem,
):
    first_col = lax.axis_index("hid") * COLS

    @pl.when(pl.program_id(0) == 0)
    def _():
        loads = [
            pltpu.make_async_copy(src, dst, local_sem.at[k])
            for k, (src, dst) in enumerate(
                ((row_hbm, row_ref), (col_hbm, col_ref))
            )
        ]
        for load in loads:
            load.start()
        for load in loads:
            load.wait()
        for c in range(COLS):
            for g in range(4):
                turned[c, :, g * 128 : (g + 1) * 128] = hidden_ref[g, c].T

    count = count_ref[0]
    for k in range(STEP):
        s = pl.program_id(0) * STEP + k
        row = row_ref[s]
        col = col_ref[s] - first_col
        rows = jnp.concatenate([grads_ref[g, row] for g in range(4)], axis=0)
        value = dot(turned[col], rows, ((1,), (0,)))
        out_ref[k] = jnp.where(s < count, value, 0.0)
        in_ref[k] = total_ref[s].astype(F32)

    @pl.when(pl.program_id(0) == 0)
    def _():
        sums = []
        for a in range(2):
            both = sums_ref[0, a].astype(F32) + sums_ref[1, a].astype(F32)
            sums.append(
                jnp.concatenate(
                    [both[p // 8, 2 * (p % 8) : 2 * (p % 8) + 2, :] for p in range(64)], axis=1
                )
            )
        x_hat, inv_std = layer_norm(act_ref)
        layer_ref[...] = (act_ref[...].astype(F32) + sums[0]).astype(BF16)
        scaled = sums[1] * gain_ref[...]
        mean_g = jnp.sum(scaled, axis=-1, keepdims=True) * (1.0 / WIDTH)
        mean_gx = jnp.sum(scaled * x_hat, axis=-1, keepdims=True) * (1.0 / WIDTH)
        gin_ref[...] = (
            inv_std * (scaled - mean_g - x_hat * mean_gx) + grad_ref[...].astype(F32)
        ).astype(BF16)


def finish(rows, cols, count, act, gain, grad, sums, hidden, grads, totals):
    vmem = pl.BlockSpec(memory_space=pltpu.VMEM)
    hbm = pl.BlockSpec(memory_space=pltpu.HBM)
    pin = functools.partial(pltpu.with_memory_space_constraint, memory_space=pltpu.HBM)
    block = pl.BlockSpec((STEP, 128, 128), lambda i: (i, 0, 0))
    line = pl.BlockSpec((2, WIDTH), lambda i: (0, 0))
    shape = jax.ShapeDtypeStruct((SLOTS, 128, 128), F32)
    narrow = jax.ShapeDtypeStruct((2, WIDTH), BF16)
    return pl.pallas_call(
        finish_kernel,
        grid=(SLOTS // STEP,),
        out_shape=(narrow, narrow, shape, shape),
        in_specs=[hbm] * 2 + [pl.BlockSpec(memory_space=pltpu.SMEM)] + [vmem] * 7,
        out_specs=(line, line, block, block),
        scratch_shapes=[
            pltpu.VMEM((COLS, 128, 512), BF16),
            pltpu.SMEM((SLOTS,), jnp.int32),
            pltpu.SMEM((SLOTS,), jnp.int32),
            pltpu.SemaphoreType.DMA((2,)),
        ],
        compiler_params=pltpu.CompilerParams(vmem_limit_bytes=8 << 20),
        name="block_gradients",
    )(pin(rows), pin(cols), count, act, gain, grad, sums, hidden, grads, totals)


def local(activations, ln_gain, in_blocks, out_blocks, block_row, block_col, block_count, grad_out):
    gain = ln_gain.reshape(1, WIDTH)
    everything, outer_y, outer_x = gather(activations, gain, grad_out)
    sums, parts, hidden = compute(
        block_row, block_col, block_count, everything.reshape(2, 64, 128, 128), in_blocks, out_blocks
    )
    row_sums, totals, hiddens, grads = reduce(
        sums.reshape(2, 4, 2, 8, 2, 4, 16, 128), parts, hidden, everything, outer_y, outer_x
    )
    return finish(
        block_row, block_col, block_count, activations, gain, grad_out, row_sums,
        hiddens, grads.reshape(4, 64, 128, 128), totals,
    )


def solution(mesh):
    rows, blocks, slots = P(("seq", "hid"), None), P("hid", None, None), P("hid")
    in_specs = (rows, P(), blocks, blocks, slots, slots, slots, rows)
    out_specs = (rows, rows, blocks, blocks)
    return jax.shard_map(local, mesh=mesh, in_specs=in_specs, out_specs=out_specs, check_vma=False)
```

```python
import functools

import jax
import jax.numpy as jnp
from jax import lax
from jax.experimental import pallas as pl
from jax.experimental.pallas import tpu as pltpu
from jax.sharding import PartitionSpec as P

F32 = jnp.float32
BF16 = jnp.bfloat16
MESH = pl.DeviceIdType.MESH
WIDTH = 8192
SLOTS = 36
COLS = 3
CHUNK = 1
CHUNKS = SLOTS // CHUNK
LAG = 5


def place():
    seq, hid = lax.axis_index("seq"), lax.axis_index("hid")
    return seq, hid // 32, (hid // 8) % 4, (hid // 2) % 4, hid % 2


def device(seq, zh, x, y, core):
    return (seq, zh * 32 + x * 8 + y * 2 + core)


def remote(src, dst, send, recv, to):
    return pltpu.make_async_remote_copy(
        src_ref=src, dst_ref=dst, send_sem=send, recv_sem=recv, device_id=to, device_id_type=MESH
    )


def meet(peers):
    barrier = pltpu.get_barrier_semaphore()
    for peer in peers:
        pl.semaphore_signal(barrier, inc=1, device_id=peer, device_id_type=MESH)
    pl.semaphore_wait(barrier, len(peers))


def octet_peers(seq, zh, x, y, core):
    offsets = [(dx, dc) for dx in (2, 1, 3, 0) for dc in (0, 1) if (dx, dc) != (0, 0)]
    return [((x + dx) % 4, (core + dc) % 2) for dx, dc in offsets]


def layer_norm(act_ref):
    values = act_ref[...].astype(F32)
    mean = jnp.sum(values, axis=-1, keepdims=True) * (1.0 / WIDTH)
    centered = values - mean
    variance = jnp.sum(centered * centered, axis=-1, keepdims=True) * (1.0 / WIDTH)
    inv_std = lax.rsqrt(variance + 1e-05)
    return centered * inv_std, inv_std


def gather_kernel(
    act_hbm, gain_hbm, grad_hbm, all_ref, outer_y, outer_x,
    act_ref, gain_ref, grad_ref, wide, packed, landed,
    local_sem, a2a_send, a2a_recv, z_send, z_recv, s1_send, s1_recv,
    s2_send, s2_recv, fw_send, fw_recv, sw_send, sw_recv, o_send, o_recv,
):
    seq, zh, x, y, core = place()
    me = x * 2 + core
    octet = octet_peers(seq, zh, x, y, core)
    xs = [(x + d) % 4 for d in (1, 3, 2)]
    ys = [(y + d) % 4 for d in (1, 3, 2)]
    planes = (zh, 1 - zh)
    sibling = device(seq, zh, x, y, 1 - core)
    loads = [
        pltpu.make_async_copy(src, dst, local_sem.at[k])
        for k, (src, dst) in enumerate(
            ((act_hbm, act_ref), (gain_hbm, gain_ref), (grad_hbm, grad_ref))
        )
    ]
    for load in loads:
        load.start()
    targets = [(0, px, pc) for px, pc in octet] + [(1, px, pc) for px, pc in octet]
    targets.append((1, x, core))
    peers = [device(seq, planes[f], px, y, pc) for f, px, pc in targets]
    peers += [device(seq, zh, x, py, core) for py in ys]
    peers += [device((seq + d) % 4, zh, x, y, core) for d in (1, 2, 3)]
    barrier = pltpu.get_barrier_semaphore()
    for peer in peers:
        pl.semaphore_signal(barrier, inc=1, device_id=peer, device_id_type=MESH)
    for load in loads:
        load.wait()
    x_hat, _ = layer_norm(act_ref)
    for a, rows in enumerate((x_hat * gain_ref[...], grad_ref[...].astype(F32))):
        for p in range(64):
            wide[a, 2 * p : 2 * p + 2, :] = rows[:, p * 128 : (p + 1) * 128]
        packed[a] = wide[a].astype(BF16).reshape(8, 16, 128)
    pl.semaphore_wait(barrier, len(peers))
    near, far = [], []
    for k in [*range(7, 15), *range(7)]:
        f, px, pc = targets[k]
        copy = remote(
            packed.at[:, px * 2 + pc], landed.at[zh, :, me], a2a_send.at[k], a2a_recv.at[k],
            peers[k],
        )
        copy.start()
        (far if f else near).append(copy)
    landed[zh, :, me] = packed[:, me]

    def relayout(zp):
        for a in range(2):
            wide[a] = landed[zp, a].astype(F32).reshape(128, 128)
            for p in range(8):
                first = wide[a, pl.ds(2 * p, 8, stride=16), :]
                second = wide[a, pl.ds(2 * p + 1, 8, stride=16), :]
                all_ref[a, x, core, p, zp, y] = jnp.concatenate([first, second], axis=0).astype(BF16)

    stage_ones, stage_twos, forwards, swaps, lines, outers = {}, {}, {}, [], [], []

    def stage_one(f):
        zp = planes[f]
        for a in (0, 1):
            block = all_ref.at[a, x, core, :, zp, y]
            out = []
            for d in range(3):
                to = device(seq, zh, xs[d], y, core) if a == 0 else device(seq, zh, x, ys[d], core)
                out.append(remote(block, block, s1_send.at[f, a, d], s1_recv.at[f, a, d], to))
                out[-1].start()
            stage_ones[f, a] = out

    def piece(f, other, nx, ny):
        return outer_x.at[other, nx] if f else outer_y.at[other, :, ny]

    def along_z(f):
        zp = planes[f]
        for d in (1, 2, 3):
            lines.append(
                remote(all_ref.at[1, x, core, :, zp, y], piece(f, seq, x, y),
                       z_send.at[f, d - 1], z_recv.at[f, d - 1],
                       device((seq + d) % 4, zh, x, y, core))
            )
            lines[-1].start()

    def outer_first():
        for f in range(2):
            for k in range(3):
                lines[3 * f + 2 - k].wait_recv()
                block = piece(f, (seq + k + 1) % 4, x, y)
                for d in range(3):
                    to = device(seq, zh, xs[d], y, core) if f else device(seq, zh, x, ys[d], core)
                    outers.append(
                        remote(block, block, o_send.at[f, k, d], o_recv.at[f, k, d], to)
                    )
                    outers[-1].start()

    def part(f, a, nx, ny, half):
        zp = planes[f]
        if a == 0:
            if half is None:
                return all_ref.at[0, :, core, :, zp, ny]
            return all_ref.at[0, pl.ds(2 * half, 2), core, :, zp, ny]
        if half is None:
            return all_ref.at[1, nx, core, :, zp]
        return all_ref.at[1, nx, core, pl.ds(4 * half, 4), zp]

    def ahead(a, d):
        if a == 0:
            return device(seq, zh, x, ys[d], core)
        return device(seq, zh, xs[d], y, core)

    def swap(f, a, k, block):
        copy = remote(block, block, sw_send.at[f, a, k], sw_recv.at[f, a, k], sibling)
        copy.start()
        swaps.append(copy)

    def stage_two(f):
        for a in (0, 1):
            for copy in stage_ones[f, a]:
                copy.wait_recv()
            for n in range(2):
                for d in range(2):
                    half = n if d == 0 else 1 - n
                    block = part(f, a, x, y, half)
                    stage_twos[f, a, d, half] = remote(
                        block, block, s2_send.at[f, a, d, half], s2_recv.at[f, a, d, half],
                        ahead(a, d),
                    )
                    stage_twos[f, a, d, half].start()
        for a in (0, 1):
            swap(f, a, 0, part(f, a, x, y, None))

    def forward(f):
        for a in (0, 1):
            out = []
            for d in range(2):
                stage_twos[f, a, d, d].wait_recv()
                block = part(f, a, xs[1 - d], ys[1 - d], d)
                out.append(
                    remote(block, block, fw_send.at[f, a, d], fw_recv.at[f, a, d], ahead(a, d))
                )
                out[-1].start()
            forwards[f, a] = out
        for a in (0, 1):
            for d in range(2):
                stage_twos[f, a, d, 1 - d].wait_recv()
                swap(f, a, 1 + d, part(f, a, xs[1 - d], ys[1 - d], None))

    def finish(f):
        for a in (0, 1):
            for copy in forwards[f, a]:
                copy.wait_recv()
            swap(f, a, 3, part(f, a, xs[2], ys[2], None))

    for copy in near:
        copy.wait_recv()
    relayout(zh)
    stage_one(0)
    for copy in far:
        copy.wait_recv()
    relayout(1 - zh)
    stage_one(1)
    stage_two(0)
    along_z(0)
    along_z(1)
    stage_two(1)
    forward(0)
    forward(1)
    outer_first()
    finish(0)
    finish(1)
    for copy in swaps + outers:
        copy.wait_recv()
    for copy in near + far + lines + swaps + outers:
        copy.wait_send()
    for copy in stage_twos.values():
        copy.wait_send()
    for group in (stage_ones, forwards):
        for copies in group.values():
            for copy in copies:
                copy.wait_send()


def gather(act, gain, grad):
    vmem = pl.BlockSpec(memory_space=pltpu.VMEM)
    hbm = pl.BlockSpec(memory_space=pltpu.HBM)
    dma = pltpu.SemaphoreType.DMA
    return pl.pallas_call(
        gather_kernel,
        out_shape=(
            jax.ShapeDtypeStruct((2, 4, 2, 8, 2, 4, 16, 128), BF16),
            jax.ShapeDtypeStruct((4, 8, 4, 16, 128), BF16),
            jax.ShapeDtypeStruct((4, 4, 8, 16, 128), BF16),
        ),
        in_specs=[hbm] * 3,
        out_specs=(vmem, vmem, vmem),
        scratch_shapes=[
            pltpu.VMEM((2, WIDTH), BF16),
            pltpu.VMEM((1, WIDTH), F32),
            pltpu.VMEM((2, WIDTH), BF16),
            pltpu.VMEM((2, 128, 128), F32),
            pltpu.VMEM((2, 8, 16, 128), BF16),
            pltpu.VMEM((2, 2, 8, 16, 128), BF16),
            dma((3,)), dma((15,)), dma((15,)), dma((2, 3)), dma((2, 3)),
            dma((2, 2, 3)), dma((2, 2, 3)), dma((2, 2, 2, 2)), dma((2, 2, 2, 2)),
            dma((2, 2, 2)), dma((2, 2, 2)), dma((2, 2, 4)), dma((2, 2, 4)),
            dma((2, 3, 3)), dma((2, 3, 3)),
        ],
        compiler_params=pltpu.CompilerParams(
            collective_id=1, has_side_effects=True, vmem_limit_bytes=12 << 20
        ),
        cost_estimate=pl.CostEstimate(flops=0, bytes_accessed=64 << 20, transcendentals=0),
        name="gather_rows",
    )(*(pltpu.with_memory_space_constraint(v, pltpu.HBM) for v in (act, gain, grad)))


def dot(a, b, dims):
    return lax.dot_general(a, b, (dims, ((), ())), preferred_element_type=F32)


GROUP = 36


def compute_kernel(
    row_hbm, col_hbm, count_ref, all_ref, in_hbm, out_hbm, total, hidden, grad_pre,
    row_ref, col_ref, in_ref, out_ref, pre, grad_hidden, local_sem,
):
    first_col = lax.axis_index("hid") * COLS
    loads = [
        pltpu.make_async_copy(src, dst, local_sem.at[k])
        for k, (src, dst) in enumerate(
            ((row_hbm, row_ref), (col_hbm, col_ref), (in_hbm, in_ref), (out_hbm, out_ref))
        )
    ]
    for load in loads:
        load.start()

    def clear(p, _):
        total[0, p] = jnp.zeros((128, 128), F32)
        total[1, p] = jnp.zeros((128, 128), F32)
        return 0

    lax.fori_loop(0, 64, clear, 0)
    pre[...] = jnp.zeros_like(pre)
    grad_hidden[...] = jnp.zeros_like(grad_hidden)
    for load in loads:
        load.wait()
    count = count_ref[0]

    def up(g, _):
        parts = []
        for k in range(GROUP):
            s = g * GROUP + k
            row = row_ref[s]
            live = s < count
            one = dot(all_ref[0, row], in_ref[s], ((1,), (0,)))
            two = dot(all_ref[1, row], out_ref[s], ((1,), (1,)))
            parts.append((s, jnp.where(live, one, 0.0), jnp.where(live, two, 0.0)))
        for s, one, two in parts:
            col = col_ref[s] - first_col
            pre[col] += one
            grad_hidden[col] += two
        return 0

    lax.fori_loop(0, SLOTS // GROUP, up, 0)
    for c in range(COLS):
        value = pre[c]
        sig = jax.nn.sigmoid(value)
        hidden[c] = (value * sig).astype(BF16)
        grad_pre[c] = (grad_hidden[c] * sig * (1.0 + value * (1.0 - sig))).astype(BF16)

    def down(g, _):
        parts = []
        for k in range(GROUP):
            s = g * GROUP + k
            row = row_ref[s]
            col = col_ref[s] - first_col
            live = s < count
            h, gp = hidden[col], grad_pre[col]
            one = dot(h, out_ref[s], ((1,), (0,)))
            two = dot(gp, in_ref[s], ((1,), (1,)))
            parts.append((s, row, jnp.where(live, one, 0.0), jnp.where(live, two, 0.0)))
        for s, row, one, two in parts:
            total[0, row] += one
            total[1, row] += two
        return 0

    lax.fori_loop(0, SLOTS // GROUP, down, 0)


def compute(rows, cols, count, everything, in_blocks, out_blocks):
    vmem = pl.BlockSpec(memory_space=pltpu.VMEM)
    hbm = pl.BlockSpec(memory_space=pltpu.HBM)
    pin = functools.partial(pltpu.with_memory_space_constraint, memory_space=pltpu.HBM)
    return pl.pallas_call(
        compute_kernel,
        out_shape=(
            jax.ShapeDtypeStruct((2, 64, 128, 128), F32),
            jax.ShapeDtypeStruct((COLS, 128, 128), BF16),
            jax.ShapeDtypeStruct((COLS, 128, 128), BF16),
        ),
        in_specs=[hbm] * 2 + [pl.BlockSpec(memory_space=pltpu.SMEM)] + [vmem] + [hbm] * 2,
        out_specs=(vmem, vmem, vmem),
        scratch_shapes=[
            pltpu.SMEM((SLOTS,), jnp.int32),
            pltpu.SMEM((SLOTS,), jnp.int32),
            pltpu.VMEM((SLOTS, 128, 128), BF16),
            pltpu.VMEM((SLOTS, 128, 128), BF16),
            pltpu.VMEM((COLS, 128, 128), F32),
            pltpu.VMEM((COLS, 128, 128), F32),
            pltpu.SemaphoreType.DMA((4,)),
        ],
        compiler_params=pltpu.CompilerParams(vmem_limit_bytes=24 << 20),
        name="block_products",
    )(pin(rows), pin(cols), count, everything, pin(in_blocks), pin(out_blocks))


def reduce_kernel(
    row_ref, col_ref, count_ref, wide_ref, hidden_ref, gp_ref, all_ref, blocks_ref, outer_y, outer_x,
    rows, total_ref, hiddens_ref, grads_ref, sums_ref, part_ref,
    swap_a, swap_b, half_a, half_b, near_a, near_b, quart_a, quart_b, far_a, far_b,
    wide, back,
    end_in, mid_own, mid_in,
    sw_send, sw_recv, n_send, n_recv, f_send, f_recv, b_send, b_recv,
    e_send, e_recv, m_send, m_recv, t_send, t_recv,
    h_send, h_recv, own_sem, ob_send, ob_recv, of_send, of_recv, os_send, os_recv,
):
    seq, zh, x, y, core = place()
    me = x * 2 + core
    octet = octet_peers(seq, zh, x, y, core)
    sibling = device(seq, zh, x, y, 1 - core)
    beside = device(seq + 1 - 2 * (seq % 2), zh, x, y, core)
    across = device(3 - seq, zh, x, y, core)
    is_mid = jnp.logical_or(seq == 1, seq == 2)
    is_end = jnp.logical_or(seq == 0, seq == 3)
    targets = [(zh, px, pc) for px, pc in octet] + [(1 - zh, px, pc) for px, pc in octet]
    targets.append((1 - zh, x, core))
    peers = [device(seq, zt, px, y, pc) for zt, px, pc in targets]
    peers += [device(seq, zh, x, (y + d) % 4, core) for d in (1, 2, 3)]
    peers += [device((seq + d) % 4, zh, x, y, core) for d in (1, 2, 3)]
    barrier = pltpu.get_barrier_semaphore()
    for peer in peers:
        pl.semaphore_signal(barrier, inc=1, device_id=peer, device_id_type=MESH)
    others = [(seq + d) % 4 for d in (1, 2, 3)]
    xs = [(x + d) % 4 for d in (1, 3, 2)]
    ys = [(y + d) % 4 for d in (1, 3, 2)]

    own_rows = pltpu.make_async_copy(all_ref.at[1], grads_ref.at[seq], own_sem)
    own_rows.start()

    def narrow(v, _):
        for c in range(2):
            for p in range(8):
                sums_ref[0, v, c, p] = wide_ref[0, v, c, p].astype(BF16)
                sums_ref[1, v, c, p] = wide_ref[1, v, c, p].astype(BF16)
        return 0

    lax.fori_loop(0, 4, narrow, 0)
    first_col = lax.axis_index("hid") * COLS
    count = count_ref[0]

    def product(g, _):
        for k in range(12):
            s = g * 12 + k
            row = jnp.clip(row_ref[s], 0, 63)
            col = jnp.clip(col_ref[s] - first_col, 0, COLS - 1)
            value = dot(blocks_ref[0, row], gp_ref[col], ((0,), (0,)))
            part_ref[s] = jnp.where(s < count, value, 0.0).astype(BF16)
        return 0

    lax.fori_loop(0, SLOTS // 12, product, 0)
    hiddens_ref[seq] = hidden_ref[...]
    for other in others:
        for n in range(8):
            grads_ref[other, x, core, n, zh] = outer_y[other, n]
        for n in range(4):
            grads_ref[other, n, core, :, 1 - zh, y] = outer_x[other, n]
    pl.semaphore_wait(barrier, len(peers))

    def chunk(ref, k):
        return ref.at[pl.ds(k * CHUNK, CHUNK)]

    def end_copy(k):
        return remote(chunk(part_ref, k), chunk(end_in, k), e_send.at[k], e_recv.at[k], beside)

    def mid_copy(k):
        return remote(chunk(mid_own, k), chunk(mid_in, k), m_send.at[k], m_recv.at[k], across)

    def total_copy(k):
        return remote(chunk(total_ref, k), chunk(total_ref, k), t_send.at[k], t_recv.at[k], beside)

    def mid_first(k):
        end_copy(k).wait_recv()
        for j in range(CHUNK):
            s = k * CHUNK + j
            mid_own[s] = (end_in[s].astype(F32) + part_ref[s].astype(F32)).astype(BF16)
        mid_copy(k).start()

    def mid_second(k):
        mid_copy(k).wait_recv()
        for j in range(CHUNK):
            s = k * CHUNK + j
            total_ref[s] = (mid_own[s].astype(F32) + mid_in[s].astype(F32)).astype(BF16)
        total_copy(k).start()

    done = [0]

    def chain(steps):
        start, stop = done[0], min(done[0] + steps, CHUNKS + LAG)
        done[0] = stop

        @pl.when(is_mid)
        def _():
            def step(k, _):
                @pl.when(k < CHUNKS)
                def _():
                    mid_first(k)

                @pl.when(k >= LAG)
                def _():
                    mid_second(k - LAG)

                return 0

            lax.fori_loop(start, stop, step, 0)

    order = (2, 1, 3, 0)
    swaps = []
    for d in order:
        pair = (
            remote(sums_ref.at[0, (x + d) % 4, 1 - core], swap_a.at[d],
                   sw_send.at[0, d], sw_recv.at[0, d], sibling),
            remote(sums_ref.at[1, :, 1 - core, :, :, (y + d) % 4], swap_b.at[d],
                   sw_send.at[1, d], sw_recv.at[1, d], sibling),
        )
        for copy in pair:
            copy.start()
        swaps.append(pair)

    near_end = seq + 1 - 2 * (seq % 2)
    mid = 3 - seq
    far_end = mid + 1 - 2 * (mid % 2)

    def hidden_copy(source, k, to):
        block = hiddens_ref.at[source]
        return remote(block, block, h_send.at[k], h_recv.at[source], to)

    outer_b, outer_f, outer_s = [], [], []
    planes = (zh, 1 - zh)
    def outer_block(other, f, nx, ny, half):
        if f:
            if half is None:
                return grads_ref.at[other, :, core, :, planes[1], ny]
            return grads_ref.at[other, pl.ds(2 * half, 2), core, :, planes[1], ny]
        if half is None:
            return grads_ref.at[other, nx, core, :, planes[0]]
        return grads_ref.at[other, nx, core, pl.ds(4 * half, 4), planes[0]]

    def outer_to(f, d):
        return device(seq, zh, x, ys[d], core) if f else device(seq, zh, xs[d], y, core)

    def outer_swap(k, f, n, block):
        copy = remote(block, block, os_send.at[k, f, n], os_recv.at[k, f, n], sibling)
        copy.start()
        outer_s.append(copy)

    def outer_second(k):
        other = others[k]
        for f in range(2):
            block = outer_block(other, f, x, y, None)
            for d in range(2):
                outer_b.append(
                    remote(block, block, ob_send.at[k, f, d], ob_recv.at[k, f, d], outer_to(f, d))
                )
                outer_b[-1].start()
        for f in range(2):
            outer_swap(k, f, 0, outer_block(other, f, x, y, None))

    def outer_forward(k):
        other = others[k]
        for f in range(2):
            for d in range(2):
                outer_b[4 * k + 2 * f + d].wait_recv()
                block = outer_block(other, f, xs[1 - d], ys[1 - d], d)
                outer_f.append(
                    remote(block, block, of_send.at[k, f, d], of_recv.at[k, f, d], outer_to(f, d))
                )
                outer_f[-1].start()
            for d in range(2):
                outer_swap(k, f, 1 + d, outer_block(other, f, xs[1 - d], ys[1 - d], None))

    def outer_finish(k):
        other = others[k]
        for f in range(2):
            for d in range(2):
                outer_f[4 * k + 2 * f + d].wait_recv()
            outer_swap(k, f, 3, outer_block(other, f, xs[2], ys[2], None))

    @pl.when(is_end)
    def _():
        def step(k, _):
            end_copy(k).start()
            return 0

        lax.fori_loop(0, 12, step, 0)
        hidden_copy(seq, 0, beside).start()
        lax.fori_loop(12, CHUNKS, step, 0)

    @pl.when(is_mid)
    def _():
        hidden_copy(seq, 0, beside).start()
        hidden_copy(seq, 1, across).start()

    nears = []
    for d, (copy_a, copy_b) in zip(order[:3], swaps):
        copy_a.wait_recv()

        def add_a(p, _):
            half_a[d, p] = (
                sums_ref[0, (x + d) % 4, core, p].astype(F32) + swap_a[d, p].astype(F32)
            ).astype(BF16)
            return 0

        lax.fori_loop(0, 8, add_a, 0)
        nears.append(
            remote(half_a.at[d], near_a.at[d], n_send.at[0, d], n_recv.at[0, d],
                   device(seq, zh, (x + d) % 4, y, core))
        )
        nears[-1].start()
        copy_b.wait_recv()

        def add_b(p, _):
            for v in range(4):
                half_b[d, v, p] = (
                    sums_ref[1, v, core, p, :, (y + d) % 4].astype(F32)
                    + swap_b[d, v, p].astype(F32)
                ).astype(BF16)
            return 0

        lax.fori_loop(0, 8, add_b, 0)
        nears.append(
            remote(half_b.at[d], near_b.at[d], n_send.at[1, d], n_recv.at[1, d],
                   device(seq, zh, x, (y + d) % 4, core))
        )
        nears[-1].start()
        chain(2)
    for copy in swaps[3]:
        copy.wait_recv()
    for copy in nears:
        chain(3)
        copy.wait_recv()

    @pl.when(is_mid)
    def _():
        hidden_copy(near_end, 0, beside).wait_recv()
        hidden_copy(near_end, 2, across).start()
        hidden_copy(mid, 0, beside).wait_recv()
        hidden_copy(mid, 3, beside).start()


    def sum_a(p, _):
        value = sums_ref[0, x, core, p].astype(F32) + swap_a[0, p].astype(F32)
        for d in (1, 2, 3):
            value += near_a[d, p].astype(F32)
        quart_a[p] = value.astype(BF16)
        return 0

    lax.fori_loop(0, 8, sum_a, 0)
    fars = []
    for d in order[:3]:
        fars.append(
            remote(quart_a.at[:, :, (y + d) % 4], far_a.at[d], f_send.at[0, d], f_recv.at[0, d],
                   device(seq, zh, x, (y + d) % 4, core))
        )
        fars[-1].start()

    def sum_b(p, _):
        for v in range(4):
            value = sums_ref[1, v, core, p, :, y].astype(F32) + swap_b[0, v, p].astype(F32)
            for d in (1, 2, 3):
                value += near_b[d, v, p].astype(F32)
            quart_b[v, p] = value.astype(BF16)
        return 0

    lax.fori_loop(0, 8, sum_b, 0)
    for d in order[:3]:
        fars.append(
            remote(quart_b.at[(x + d) % 4], far_b.at[d], f_send.at[1, d], f_recv.at[1, d],
                   device(seq, zh, (x + d) % 4, y, core))
        )
        fars[-1].start()
    outer_second(0)
    outer_second(1)
    outer_second(2)
    for copy in fars:
        chain(1)
        copy.wait_recv()

    def sum_far(p, _):
        one = quart_a[p, :, y].astype(F32)
        two = quart_b[x, p].astype(F32)
        for d in (1, 2, 3):
            one += far_a[d, p].astype(F32)
            two += far_b[d, p].astype(F32)
        for zt in range(2):
            for a, value in enumerate((one[zt], two[zt])):
                wide[zt, a, pl.ds(2 * p, 8, stride=16), :] = value[0:8]
                wide[zt, a, pl.ds(2 * p + 1, 8, stride=16), :] = value[8:16]
        return 0

    lax.fori_loop(0, 8, sum_far, 0)
    for zt in range(2):
        for a in range(2):
            back[zt, a] = wide[zt, a].astype(BF16).reshape(8, 16, 128)
    backs = []
    for k, (zt, px, pc) in enumerate(targets):
        backs.append(
            remote(back.at[zt, :, px * 2 + pc], rows.at[zh, :, me], b_send.at[k], b_recv.at[k],
                   device(seq, zt, px, y, pc))
        )
        backs[-1].start()
    rows[zh, :, me] = back[zh, :, me]
    outer_forward(0)
    chain(5)

    @pl.when(is_mid)
    def _():
        hidden_copy(far_end, 0, beside).wait_recv()
        hidden_copy(far_end, 4, beside).start()

    outer_forward(1)
    chain(2)
    for copy in backs:
        copy.wait_recv()
    outer_forward(2)
    chain(5)
    for k in range(3):
        chain(1)
        outer_finish(k)
    chain(CHUNKS + LAG)

    @pl.when(is_mid)
    def _():
        def step(k, _):
            mid_copy(k).wait_send()
            total_copy(k).wait_send()
            return 0

        lax.fori_loop(0, CHUNKS, step, 0)
        for k in range(5):
            hidden_copy(seq, k, beside).wait_send()

    @pl.when(is_end)
    def _():
        def step(k, _):
            end_copy(k).wait_send()
            total_copy(k).wait_recv()
            return 0

        lax.fori_loop(0, CHUNKS, step, 0)
        hidden_copy(seq, 0, beside).wait_send()
        for source in (near_end, mid, far_end):
            hidden_copy(source, 0, beside).wait_recv()

    for copy in outer_s:
        copy.wait_recv()
    own_rows.wait()
    for pair in swaps:
        for copy in pair:
            copy.wait_send()
    for copy in nears + fars + backs + outer_b + outer_f + outer_s:
        copy.wait_send()


def reduce(slot_rows, slot_cols, count, sums, hidden, grad_pre, everything, outer_y, outer_x):
    vmem = pl.BlockSpec(memory_space=pltpu.VMEM)
    dma = pltpu.SemaphoreType.DMA
    slot = (SLOTS, 128, 128)
    return pl.pallas_call(
        reduce_kernel,
        out_shape=(
            jax.ShapeDtypeStruct((2, 2, 8, 16, 128), BF16),
            jax.ShapeDtypeStruct(slot, BF16),
            jax.ShapeDtypeStruct((4, COLS, 128, 128), BF16),
            jax.ShapeDtypeStruct((4, 4, 2, 8, 2, 4, 16, 128), BF16),
        ),
        in_specs=[pl.BlockSpec(memory_space=pltpu.SMEM)] * 3 + [vmem] * 7,
        out_specs=(vmem,) * 4,
        scratch_shapes=[
            pltpu.VMEM((2, 4, 2, 8, 2, 4, 16, 128), BF16),
            pltpu.VMEM(slot, BF16),
            pltpu.VMEM((4, 8, 2, 4, 16, 128), BF16),
            pltpu.VMEM((4, 4, 8, 2, 16, 128), BF16),
            pltpu.VMEM((4, 8, 2, 4, 16, 128), BF16),
            pltpu.VMEM((4, 4, 8, 2, 16, 128), BF16),
            pltpu.VMEM((4, 8, 2, 4, 16, 128), BF16),
            pltpu.VMEM((4, 4, 8, 2, 16, 128), BF16),
            pltpu.VMEM((8, 2, 4, 16, 128), BF16),
            pltpu.VMEM((4, 8, 2, 16, 128), BF16),
            pltpu.VMEM((4, 8, 2, 16, 128), BF16),
            pltpu.VMEM((4, 8, 2, 16, 128), BF16),
            pltpu.VMEM((2, 2, 128, 128), F32),
            pltpu.VMEM((2, 2, 8, 16, 128), BF16),
            pltpu.VMEM(slot, BF16),
            pltpu.VMEM(slot, BF16),
            pltpu.VMEM(slot, BF16),
            dma((2, 4)), dma((2, 4)), dma((2, 4)), dma((2, 4)), dma((2, 4)), dma((2, 4)),
            dma((15,)), dma((15,)),
            dma((CHUNKS,)), dma((CHUNKS,)), dma((CHUNKS,)), dma((CHUNKS,)),
            dma((CHUNKS,)), dma((CHUNKS,)),
            dma((5,)), dma((4,)), dma, dma((3, 2, 2)), dma((3, 2, 2)),
            dma((3, 2, 2)), dma((3, 2, 2)), dma((3, 2, 4)), dma((3, 2, 4)),
        ],
        compiler_params=pltpu.CompilerParams(
            collective_id=2, has_side_effects=True, vmem_limit_bytes=24 << 20
        ),
        cost_estimate=pl.CostEstimate(flops=0, bytes_accessed=64 << 20, transcendentals=0),
        name="reduce_sums",
    )(
        slot_rows, slot_cols, count, sums, hidden, grad_pre,
        everything, everything.reshape(2, 64, 128, 128), outer_y, outer_x,
    )


STEP = 36


def finish_kernel(
    row_hbm, col_hbm, count_ref, act_ref, gain_ref, grad_ref, sums_ref,
    hidden_ref, grads_ref, total_ref, layer_ref, gin_ref, in_ref, out_ref,
    turned, row_ref, col_ref, local_sem,
):
    first_col = lax.axis_index("hid") * COLS

    @pl.when(pl.program_id(0) == 0)
    def _():
        loads = [
            pltpu.make_async_copy(src, dst, local_sem.at[k])
            for k, (src, dst) in enumerate(
                ((row_hbm, row_ref), (col_hbm, col_ref))
            )
        ]
        for load in loads:
            load.start()
        for load in loads:
            load.wait()
        for c in range(COLS):
            for g in range(4):
                turned[c, :, g * 128 : (g + 1) * 128] = hidden_ref[g, c].T

    count = count_ref[0]
    for k in range(STEP):
        s = pl.program_id(0) * STEP + k
        row = row_ref[s]
        col = col_ref[s] - first_col
        rows = jnp.concatenate([grads_ref[g, row] for g in range(4)], axis=0)
        value = dot(turned[col], rows, ((1,), (0,)))
        out_ref[k] = jnp.where(s < count, value, 0.0)
        in_ref[k] = total_ref[s].astype(F32)

    @pl.when(pl.program_id(0) == 0)
    def _():
        sums = []
        for a in range(2):
            both = sums_ref[0, a].astype(F32) + sums_ref[1, a].astype(F32)
            sums.append(
                jnp.concatenate(
                    [both[p // 8, 2 * (p % 8) : 2 * (p % 8) + 2, :] for p in range(64)], axis=1
                )
            )
        x_hat, inv_std = layer_norm(act_ref)
        layer_ref[...] = (act_ref[...].astype(F32) + sums[0]).astype(BF16)
        scaled = sums[1] * gain_ref[...]
        mean_g = jnp.sum(scaled, axis=-1, keepdims=True) * (1.0 / WIDTH)
        mean_gx = jnp.sum(scaled * x_hat, axis=-1, keepdims=True) * (1.0 / WIDTH)
        gin_ref[...] = (
            inv_std * (scaled - mean_g - x_hat * mean_gx) + grad_ref[...].astype(F32)
        ).astype(BF16)


def finish(rows, cols, count, act, gain, grad, sums, hidden, grads, totals):
    vmem = pl.BlockSpec(memory_space=pltpu.VMEM)
    hbm = pl.BlockSpec(memory_space=pltpu.HBM)
    pin = functools.partial(pltpu.with_memory_space_constraint, memory_space=pltpu.HBM)
    block = pl.BlockSpec((STEP, 128, 128), lambda i: (i, 0, 0))
    line = pl.BlockSpec((2, WIDTH), lambda i: (0, 0))
    shape = jax.ShapeDtypeStruct((SLOTS, 128, 128), F32)
    narrow = jax.ShapeDtypeStruct((2, WIDTH), BF16)
    return pl.pallas_call(
        finish_kernel,
        grid=(SLOTS // STEP,),
        out_shape=(narrow, narrow, shape, shape),
        in_specs=[hbm] * 2 + [pl.BlockSpec(memory_space=pltpu.SMEM)] + [vmem] * 7,
        out_specs=(line, line, block, block),
        scratch_shapes=[
            pltpu.VMEM((COLS, 128, 512), BF16),
            pltpu.SMEM((SLOTS,), jnp.int32),
            pltpu.SMEM((SLOTS,), jnp.int32),
            pltpu.SemaphoreType.DMA((2,)),
        ],
        compiler_params=pltpu.CompilerParams(vmem_limit_bytes=8 << 20),
        name="block_gradients",
    )(pin(rows), pin(cols), count, act, gain, grad, sums, hidden, grads, totals)


def local(activations, ln_gain, in_blocks, out_blocks, block_row, block_col, block_count, grad_out):
    gain = ln_gain.reshape(1, WIDTH)
    everything, outer_y, outer_x = gather(activations, gain, grad_out)
    sums, hidden, grad_pre = compute(
        block_row, block_col, block_count, everything.reshape(2, 64, 128, 128), in_blocks, out_blocks
    )
    row_sums, totals, hiddens, grads = reduce(
        block_row, block_col, block_count, sums.reshape(2, 4, 2, 8, 2, 4, 16, 128), hidden, grad_pre,
        everything, outer_y, outer_x,
    )
    return finish(
        block_row, block_col, block_count, activations, gain, grad_out, row_sums,
        hiddens, grads.reshape(4, 64, 128, 128), totals,
    )


def solution(mesh):
    rows, blocks, slots = P(("seq", "hid"), None), P("hid", None, None), P("hid")
    in_specs = (rows, P(), blocks, blocks, slots, slots, slots, rows)
    out_specs = (rows, rows, blocks, blocks)
    return jax.shard_map(local, mesh=mesh, in_specs=in_specs, out_specs=out_specs, check_vma=False)
```

```python
import functools

import jax
import jax.numpy as jnp
from jax import lax
from jax.experimental import pallas as pl
from jax.experimental.pallas import tpu as pltpu
from jax.sharding import PartitionSpec as P

F32 = jnp.float32
BF16 = jnp.bfloat16
MESH = pl.DeviceIdType.MESH
WIDTH = 8192
SLOTS = 36
COLS = 3
CHUNK = 1
CHUNKS = SLOTS // CHUNK
LAG = 5


def place():
    seq, hid = lax.axis_index("seq"), lax.axis_index("hid")
    return seq, hid // 32, (hid // 8) % 4, (hid // 2) % 4, hid % 2


def device(seq, zh, x, y, core):
    return (seq, zh * 32 + x * 8 + y * 2 + core)


def remote(src, dst, send, recv, to):
    return pltpu.make_async_remote_copy(
        src_ref=src, dst_ref=dst, send_sem=send, recv_sem=recv, device_id=to, device_id_type=MESH
    )


def meet(peers):
    barrier = pltpu.get_barrier_semaphore()
    for peer in peers:
        pl.semaphore_signal(barrier, inc=1, device_id=peer, device_id_type=MESH)
    pl.semaphore_wait(barrier, len(peers))


def octet_peers(seq, zh, x, y, core):
    offsets = [(dx, dc) for dx in (2, 1, 3, 0) for dc in (0, 1) if (dx, dc) != (0, 0)]
    return [((x + dx) % 4, (core + dc) % 2) for dx, dc in offsets]


def layer_norm(act_ref):
    values = act_ref[...].astype(F32)
    mean = jnp.sum(values, axis=-1, keepdims=True) * (1.0 / WIDTH)
    centered = values - mean
    variance = jnp.sum(centered * centered, axis=-1, keepdims=True) * (1.0 / WIDTH)
    inv_std = lax.rsqrt(variance + 1e-05)
    return centered * inv_std, inv_std


def gather_kernel(
    act_hbm, gain_hbm, grad_hbm, all_ref, outer_y, outer_x,
    act_ref, gain_ref, grad_ref, wide, packed, landed,
    local_sem, a2a_send, a2a_recv, z_send, z_recv, s1_send, s1_recv,
    s2_send, s2_recv, fw_send, fw_recv, sw_send, sw_recv,
):
    seq, zh, x, y, core = place()
    me = x * 2 + core
    octet = octet_peers(seq, zh, x, y, core)
    xs = [(x + d) % 4 for d in (1, 3, 2)]
    ys = [(y + d) % 4 for d in (1, 3, 2)]
    planes = (zh, 1 - zh)
    sibling = device(seq, zh, x, y, 1 - core)
    loads = [
        pltpu.make_async_copy(src, dst, local_sem.at[k])
        for k, (src, dst) in enumerate(
            ((act_hbm, act_ref), (gain_hbm, gain_ref), (grad_hbm, grad_ref))
        )
    ]
    for load in loads:
        load.start()
    targets = [(0, px, pc) for px, pc in octet] + [(1, px, pc) for px, pc in octet]
    targets.append((1, x, core))
    peers = [device(seq, planes[f], px, y, pc) for f, px, pc in targets]
    peers += [device(seq, zh, x, py, core) for py in ys]
    peers += [device((seq + d) % 4, zh, x, y, core) for d in (1, 2, 3)]
    barrier = pltpu.get_barrier_semaphore()
    for peer in peers:
        pl.semaphore_signal(barrier, inc=1, device_id=peer, device_id_type=MESH)
    for load in loads:
        load.wait()
    x_hat, _ = layer_norm(act_ref)
    for a, rows in enumerate((x_hat * gain_ref[...], grad_ref[...].astype(F32))):
        for p in range(64):
            wide[a, 2 * p : 2 * p + 2, :] = rows[:, p * 128 : (p + 1) * 128]
        packed[a] = wide[a].astype(BF16).reshape(8, 16, 128)
    pl.semaphore_wait(barrier, len(peers))
    near, far = [], []
    for k in [*range(7, 15), *range(7)]:
        f, px, pc = targets[k]
        copy = remote(
            packed.at[:, px * 2 + pc], landed.at[zh, :, me], a2a_send.at[k], a2a_recv.at[k],
            peers[k],
        )
        copy.start()
        (far if f else near).append(copy)
    landed[zh, :, me] = packed[:, me]

    def relayout(zp):
        for a in range(2):
            wide[a] = landed[zp, a].astype(F32).reshape(128, 128)
            for p in range(8):
                first = wide[a, pl.ds(2 * p, 8, stride=16), :]
                second = wide[a, pl.ds(2 * p + 1, 8, stride=16), :]
                all_ref[a, x, core, p, zp, y] = jnp.concatenate([first, second], axis=0).astype(BF16)

    stage_ones, stage_twos, forwards, swaps, lines = {}, {}, {}, [], []

    def stage_one(f):
        zp = planes[f]
        for a in (0, 1):
            block = all_ref.at[a, x, core, :, zp, y]
            out = []
            for d in range(3):
                to = device(seq, zh, xs[d], y, core) if a == 0 else device(seq, zh, x, ys[d], core)
                out.append(remote(block, block, s1_send.at[f, a, d], s1_recv.at[f, a, d], to))
                out[-1].start()
            stage_ones[f, a] = out

    def piece(f, other, nx, ny):
        return outer_x.at[other, nx] if f else outer_y.at[other, :, ny]

    def along_z(f):
        zp = planes[f]
        for d in (1, 2, 3):
            lines.append(
                remote(all_ref.at[1, x, core, :, zp, y], piece(f, seq, x, y),
                       z_send.at[f, d - 1], z_recv.at[f, d - 1],
                       device((seq + d) % 4, zh, x, y, core))
            )
            lines[-1].start()

    def part(f, a, nx, ny, half):
        zp = planes[f]
        if a == 0:
            if half is None:
                return all_ref.at[0, :, core, :, zp, ny]
            return all_ref.at[0, pl.ds(2 * half, 2), core, :, zp, ny]
        if half is None:
            return all_ref.at[1, nx, core, :, zp]
        return all_ref.at[1, nx, core, pl.ds(4 * half, 4), zp]

    def ahead(a, d):
        if a == 0:
            return device(seq, zh, x, ys[d], core)
        return device(seq, zh, xs[d], y, core)

    def swap(f, a, k, block):
        copy = remote(block, block, sw_send.at[f, a, k], sw_recv.at[f, a, k], sibling)
        copy.start()
        swaps.append(copy)

    def stage_two(f):
        for a in (0, 1):
            for copy in stage_ones[f, a]:
                copy.wait_recv()
            for n in range(2):
                for d in range(2):
                    half = n if d == 0 else 1 - n
                    block = part(f, a, x, y, half)
                    stage_twos[f, a, d, half] = remote(
                        block, block, s2_send.at[f, a, d, half], s2_recv.at[f, a, d, half],
                        ahead(a, d),
                    )
                    stage_twos[f, a, d, half].start()
        for a in (0, 1):
            swap(f, a, 0, part(f, a, x, y, None))

    def forward(f):
        for a in (0, 1):
            out = []
            for d in range(2):
                stage_twos[f, a, d, d].wait_recv()
                block = part(f, a, xs[1 - d], ys[1 - d], d)
                out.append(
                    remote(block, block, fw_send.at[f, a, d], fw_recv.at[f, a, d], ahead(a, d))
                )
                out[-1].start()
            forwards[f, a] = out
        for a in (0, 1):
            for d in range(2):
                stage_twos[f, a, d, 1 - d].wait_recv()
                swap(f, a, 1 + d, part(f, a, xs[1 - d], ys[1 - d], None))

    def finish(f):
        for a in (0, 1):
            for copy in forwards[f, a]:
                copy.wait_recv()
            swap(f, a, 3, part(f, a, xs[2], ys[2], None))

    for copy in near:
        copy.wait_recv()
    relayout(zh)
    stage_one(0)
    for copy in far:
        copy.wait_recv()
    relayout(1 - zh)
    stage_one(1)
    stage_two(0)
    along_z(0)
    along_z(1)
    stage_two(1)
    forward(0)
    forward(1)
    finish(0)
    finish(1)
    for copy in swaps + lines:
        copy.wait_recv()
    for copy in near + far + lines + swaps:
        copy.wait_send()
    for copy in stage_twos.values():
        copy.wait_send()
    for group in (stage_ones, forwards):
        for copies in group.values():
            for copy in copies:
                copy.wait_send()


def gather(act, gain, grad):
    vmem = pl.BlockSpec(memory_space=pltpu.VMEM)
    hbm = pl.BlockSpec(memory_space=pltpu.HBM)
    dma = pltpu.SemaphoreType.DMA
    return pl.pallas_call(
        gather_kernel,
        out_shape=(
            jax.ShapeDtypeStruct((2, 4, 2, 8, 2, 4, 16, 128), BF16),
            jax.ShapeDtypeStruct((4, 8, 4, 16, 128), BF16),
            jax.ShapeDtypeStruct((4, 4, 8, 16, 128), BF16),
        ),
        in_specs=[hbm] * 3,
        out_specs=(vmem, vmem, vmem),
        scratch_shapes=[
            pltpu.VMEM((2, WIDTH), BF16),
            pltpu.VMEM((1, WIDTH), F32),
            pltpu.VMEM((2, WIDTH), BF16),
            pltpu.VMEM((2, 128, 128), F32),
            pltpu.VMEM((2, 8, 16, 128), BF16),
            pltpu.VMEM((2, 2, 8, 16, 128), BF16),
            dma((3,)), dma((15,)), dma((15,)), dma((2, 3)), dma((2, 3)),
            dma((2, 2, 3)), dma((2, 2, 3)), dma((2, 2, 2, 2)), dma((2, 2, 2, 2)),
            dma((2, 2, 2)), dma((2, 2, 2)), dma((2, 2, 4)), dma((2, 2, 4)),
        ],
        compiler_params=pltpu.CompilerParams(
            collective_id=1, has_side_effects=True, vmem_limit_bytes=12 << 20
        ),
        cost_estimate=pl.CostEstimate(flops=0, bytes_accessed=64 << 20, transcendentals=0),
        name="gather_rows",
    )(*(pltpu.with_memory_space_constraint(v, pltpu.HBM) for v in (act, gain, grad)))


def dot(a, b, dims):
    return lax.dot_general(a, b, (dims, ((), ())), preferred_element_type=F32)


GROUP = 36


def compute_kernel(
    row_hbm, col_hbm, count_ref, all_ref, in_hbm, out_hbm, total, hidden, grad_pre,
    row_ref, col_ref, in_ref, out_ref, pre, grad_hidden, local_sem,
):
    first_col = lax.axis_index("hid") * COLS
    loads = [
        pltpu.make_async_copy(src, dst, local_sem.at[k])
        for k, (src, dst) in enumerate(
            ((row_hbm, row_ref), (col_hbm, col_ref), (in_hbm, in_ref), (out_hbm, out_ref))
        )
    ]
    for load in loads:
        load.start()

    def clear(p, _):
        total[0, p] = jnp.zeros((128, 128), F32)
        total[1, p] = jnp.zeros((128, 128), F32)
        return 0

    lax.fori_loop(0, 64, clear, 0)
    pre[...] = jnp.zeros_like(pre)
    grad_hidden[...] = jnp.zeros_like(grad_hidden)
    for load in loads:
        load.wait()
    count = count_ref[0]

    def up(g, _):
        parts = []
        for k in range(GROUP):
            s = g * GROUP + k
            row = row_ref[s]
            live = s < count
            one = dot(all_ref[0, row], in_ref[s], ((1,), (0,)))
            two = dot(all_ref[1, row], out_ref[s], ((1,), (1,)))
            parts.append((s, jnp.where(live, one, 0.0), jnp.where(live, two, 0.0)))
        for s, one, two in parts:
            col = col_ref[s] - first_col
            pre[col] += one
            grad_hidden[col] += two
        return 0

    lax.fori_loop(0, SLOTS // GROUP, up, 0)
    for c in range(COLS):
        value = pre[c]
        sig = jax.nn.sigmoid(value)
        hidden[c] = (value * sig).astype(BF16)
        grad_pre[c] = (grad_hidden[c] * sig * (1.0 + value * (1.0 - sig))).astype(BF16)

    def down(g, _):
        parts = []
        for k in range(GROUP):
            s = g * GROUP + k
            row = row_ref[s]
            col = col_ref[s] - first_col
            live = s < count
            h, gp = hidden[col], grad_pre[col]
            one = dot(h, out_ref[s], ((1,), (0,)))
            two = dot(gp, in_ref[s], ((1,), (1,)))
            parts.append((s, row, jnp.where(live, one, 0.0), jnp.where(live, two, 0.0)))
        for s, row, one, two in parts:
            total[0, row] += one
            total[1, row] += two
        return 0

    lax.fori_loop(0, SLOTS // GROUP, down, 0)


def compute(rows, cols, count, everything, in_blocks, out_blocks):
    vmem = pl.BlockSpec(memory_space=pltpu.VMEM)
    hbm = pl.BlockSpec(memory_space=pltpu.HBM)
    pin = functools.partial(pltpu.with_memory_space_constraint, memory_space=pltpu.HBM)
    return pl.pallas_call(
        compute_kernel,
        out_shape=(
            jax.ShapeDtypeStruct((2, 64, 128, 128), F32),
            jax.ShapeDtypeStruct((COLS, 128, 128), BF16),
            jax.ShapeDtypeStruct((COLS, 128, 128), BF16),
        ),
        in_specs=[hbm] * 2 + [pl.BlockSpec(memory_space=pltpu.SMEM)] + [vmem] + [hbm] * 2,
        out_specs=(vmem, vmem, vmem),
        scratch_shapes=[
            pltpu.SMEM((SLOTS,), jnp.int32),
            pltpu.SMEM((SLOTS,), jnp.int32),
            pltpu.VMEM((SLOTS, 128, 128), BF16),
            pltpu.VMEM((SLOTS, 128, 128), BF16),
            pltpu.VMEM((COLS, 128, 128), F32),
            pltpu.VMEM((COLS, 128, 128), F32),
            pltpu.SemaphoreType.DMA((4,)),
        ],
        compiler_params=pltpu.CompilerParams(vmem_limit_bytes=24 << 20),
        name="block_products",
    )(pin(rows), pin(cols), count, everything, pin(in_blocks), pin(out_blocks))


def reduce_kernel(
    row_ref, col_ref, count_ref, wide_ref, hidden_ref, gp_ref, all_ref, blocks_ref, outer_y, outer_x,
    rows, total_ref, hiddens_ref, grads_ref, sums_ref, part_ref,
    swap_a, swap_b, half_a, half_b, near_a, near_b, quart_a, quart_b, far_a, far_b,
    wide, back,
    end_in, mid_own, mid_in,
    sw_send, sw_recv, n_send, n_recv, f_send, f_recv, b_send, b_recv,
    e_send, e_recv, m_send, m_recv, t_send, t_recv,
    h_send, h_recv, own_sem, oa_send, oa_recv, ob_send, ob_recv, of_send, of_recv, os_send, os_recv,
):
    seq, zh, x, y, core = place()
    me = x * 2 + core
    octet = octet_peers(seq, zh, x, y, core)
    sibling = device(seq, zh, x, y, 1 - core)
    beside = device(seq + 1 - 2 * (seq % 2), zh, x, y, core)
    across = device(3 - seq, zh, x, y, core)
    is_mid = jnp.logical_or(seq == 1, seq == 2)
    is_end = jnp.logical_or(seq == 0, seq == 3)
    targets = [(zh, px, pc) for px, pc in octet] + [(1 - zh, px, pc) for px, pc in octet]
    targets.append((1 - zh, x, core))
    peers = [device(seq, zt, px, y, pc) for zt, px, pc in targets]
    peers += [device(seq, zh, x, (y + d) % 4, core) for d in (1, 2, 3)]
    peers += [device((seq + d) % 4, zh, x, y, core) for d in (1, 2, 3)]
    barrier = pltpu.get_barrier_semaphore()
    for peer in peers:
        pl.semaphore_signal(barrier, inc=1, device_id=peer, device_id_type=MESH)
    others = [(seq + d) % 4 for d in (1, 2, 3)]
    xs = [(x + d) % 4 for d in (1, 3, 2)]
    ys = [(y + d) % 4 for d in (1, 3, 2)]

    own_rows = pltpu.make_async_copy(all_ref.at[1], grads_ref.at[seq], own_sem)
    own_rows.start()

    def narrow(v, _):
        for c in range(2):
            for p in range(8):
                sums_ref[0, v, c, p] = wide_ref[0, v, c, p].astype(BF16)
                sums_ref[1, v, c, p] = wide_ref[1, v, c, p].astype(BF16)
        return 0

    lax.fori_loop(0, 4, narrow, 0)
    first_col = lax.axis_index("hid") * COLS
    count = count_ref[0]

    def product(g, _):
        for k in range(12):
            s = g * 12 + k
            row = jnp.clip(row_ref[s], 0, 63)
            col = jnp.clip(col_ref[s] - first_col, 0, COLS - 1)
            value = dot(blocks_ref[0, row], gp_ref[col], ((0,), (0,)))
            part_ref[s] = jnp.where(s < count, value, 0.0).astype(BF16)
        return 0

    lax.fori_loop(0, SLOTS // 12, product, 0)
    hiddens_ref[seq] = hidden_ref[...]
    for other in others:
        for n in range(8):
            grads_ref[other, x, core, n, zh, y] = outer_y[other, n, y]
            grads_ref[other, x, core, n, 1 - zh, y] = outer_x[other, x, n]
    pl.semaphore_wait(barrier, len(peers))

    def chunk(ref, k):
        return ref.at[pl.ds(k * CHUNK, CHUNK)]

    def end_copy(k):
        return remote(chunk(part_ref, k), chunk(end_in, k), e_send.at[k], e_recv.at[k], beside)

    def mid_copy(k):
        return remote(chunk(mid_own, k), chunk(mid_in, k), m_send.at[k], m_recv.at[k], across)

    def total_copy(k):
        return remote(chunk(total_ref, k), chunk(total_ref, k), t_send.at[k], t_recv.at[k], beside)

    def mid_first(k):
        end_copy(k).wait_recv()
        for j in range(CHUNK):
            s = k * CHUNK + j
            mid_own[s] = (end_in[s].astype(F32) + part_ref[s].astype(F32)).astype(BF16)
        mid_copy(k).start()

    def mid_second(k):
        mid_copy(k).wait_recv()
        for j in range(CHUNK):
            s = k * CHUNK + j
            total_ref[s] = (mid_own[s].astype(F32) + mid_in[s].astype(F32)).astype(BF16)
        total_copy(k).start()

    done = [0]

    def chain(steps):
        start, stop = done[0], min(done[0] + steps, CHUNKS + LAG)
        done[0] = stop

        @pl.when(is_mid)
        def _():
            def step(k, _):
                @pl.when(k < CHUNKS)
                def _():
                    mid_first(k)

                @pl.when(k >= LAG)
                def _():
                    mid_second(k - LAG)

                return 0

            lax.fori_loop(start, stop, step, 0)

    order = (2, 1, 3, 0)
    swaps = []
    for d in order:
        pair = (
            remote(sums_ref.at[0, (x + d) % 4, 1 - core], swap_a.at[d],
                   sw_send.at[0, d], sw_recv.at[0, d], sibling),
            remote(sums_ref.at[1, :, 1 - core, :, :, (y + d) % 4], swap_b.at[d],
                   sw_send.at[1, d], sw_recv.at[1, d], sibling),
        )
        for copy in pair:
            copy.start()
        swaps.append(pair)

    near_end = seq + 1 - 2 * (seq % 2)
    mid = 3 - seq
    far_end = mid + 1 - 2 * (mid % 2)

    def hidden_copy(source, k, to):
        block = hiddens_ref.at[source]
        return remote(block, block, h_send.at[k], h_recv.at[source], to)

    outer_a, outer_b, outer_f, outer_s = [], [], [], []
    planes = (zh, 1 - zh)
    def outer_block(other, f, nx, ny, half):
        if f:
            if half is None:
                return grads_ref.at[other, :, core, :, planes[1], ny]
            return grads_ref.at[other, pl.ds(2 * half, 2), core, :, planes[1], ny]
        if half is None:
            return grads_ref.at[other, nx, core, :, planes[0]]
        return grads_ref.at[other, nx, core, pl.ds(4 * half, 4), planes[0]]

    def outer_to(f, d):
        return device(seq, zh, x, ys[d], core) if f else device(seq, zh, xs[d], y, core)

    def outer_swap(k, f, n, block):
        copy = remote(block, block, os_send.at[k, f, n], os_recv.at[k, f, n], sibling)
        copy.start()
        outer_s.append(copy)

    def outer_first(k):
        other = others[k]
        for f in range(2):
            block = outer_x.at[other, x] if f else outer_y.at[other, :, y]
            place_there = grads_ref.at[other, x, core, :, planes[f], y]
            for d in range(3):
                to = device(seq, zh, xs[d], y, core) if f else device(seq, zh, x, ys[d], core)
                outer_a.append(
                    remote(block, place_there, oa_send.at[k, f, d], oa_recv.at[k, f, d], to)
                )
                outer_a[-1].start()

    def outer_second(k):
        other = others[k]
        for copy in outer_a[6 * k : 6 * k + 6]:
            copy.wait_recv()
        for f in range(2):
            block = outer_block(other, f, x, y, None)
            for d in range(2):
                outer_b.append(
                    remote(block, block, ob_send.at[k, f, d], ob_recv.at[k, f, d], outer_to(f, d))
                )
                outer_b[-1].start()
        for f in range(2):
            outer_swap(k, f, 0, outer_block(other, f, x, y, None))

    def outer_forward(k):
        other = others[k]
        for f in range(2):
            for d in range(2):
                outer_b[4 * k + 2 * f + d].wait_recv()
                block = outer_block(other, f, xs[1 - d], ys[1 - d], d)
                outer_f.append(
                    remote(block, block, of_send.at[k, f, d], of_recv.at[k, f, d], outer_to(f, d))
                )
                outer_f[-1].start()
            for d in range(2):
                outer_swap(k, f, 1 + d, outer_block(other, f, xs[1 - d], ys[1 - d], None))

    def outer_finish(k):
        other = others[k]
        for f in range(2):
            for d in range(2):
                outer_f[4 * k + 2 * f + d].wait_recv()
            outer_swap(k, f, 3, outer_block(other, f, xs[2], ys[2], None))

    @pl.when(is_end)
    def _():
        def step(k, _):
            end_copy(k).start()
            return 0

        lax.fori_loop(0, 12, step, 0)
        hidden_copy(seq, 0, beside).start()
        lax.fori_loop(12, CHUNKS, step, 0)

    @pl.when(is_mid)
    def _():
        hidden_copy(seq, 0, beside).start()
        hidden_copy(seq, 1, across).start()

    nears = []
    for d, (copy_a, copy_b) in zip(order[:3], swaps):
        copy_a.wait_recv()

        def add_a(p, _):
            half_a[d, p] = (
                sums_ref[0, (x + d) % 4, core, p].astype(F32) + swap_a[d, p].astype(F32)
            ).astype(BF16)
            return 0

        lax.fori_loop(0, 8, add_a, 0, unroll=4)
        nears.append(
            remote(half_a.at[d], near_a.at[d], n_send.at[0, d], n_recv.at[0, d],
                   device(seq, zh, (x + d) % 4, y, core))
        )
        nears[-1].start()
        copy_b.wait_recv()

        def add_b(p, _):
            for v in range(4):
                half_b[d, v, p] = (
                    sums_ref[1, v, core, p, :, (y + d) % 4].astype(F32)
                    + swap_b[d, v, p].astype(F32)
                ).astype(BF16)
            return 0

        lax.fori_loop(0, 8, add_b, 0, unroll=2)
        nears.append(
            remote(half_b.at[d], near_b.at[d], n_send.at[1, d], n_recv.at[1, d],
                   device(seq, zh, x, (y + d) % 4, core))
        )
        nears[-1].start()
        chain(2)
    for k in range(3):
        outer_first(k)
    for copy in swaps[3]:
        copy.wait_recv()
    for copy in nears[0::2]:
        chain(5)
        copy.wait_recv()

    @pl.when(is_mid)
    def _():
        hidden_copy(near_end, 0, beside).wait_recv()
        hidden_copy(near_end, 2, across).start()
        hidden_copy(mid, 0, beside).wait_recv()
        hidden_copy(mid, 3, beside).start()


    def sum_a(p, _):
        value = sums_ref[0, x, core, p].astype(F32) + swap_a[0, p].astype(F32)
        for d in (1, 2, 3):
            value += near_a[d, p].astype(F32)
        quart_a[p] = value.astype(BF16)
        return 0

    lax.fori_loop(0, 8, sum_a, 0, unroll=4)
    fars = []
    for d in order[:3]:
        fars.append(
            remote(quart_a.at[:, :, (y + d) % 4], far_a.at[d], f_send.at[0, d], f_recv.at[0, d],
                   device(seq, zh, x, (y + d) % 4, core))
        )
        fars[-1].start()

    for copy in nears[1::2]:
        chain(1)
        copy.wait_recv()

    def sum_b(p, _):
        for v in range(4):
            value = sums_ref[1, v, core, p, :, y].astype(F32) + swap_b[0, v, p].astype(F32)
            for d in (1, 2, 3):
                value += near_b[d, v, p].astype(F32)
            quart_b[v, p] = value.astype(BF16)
        return 0

    lax.fori_loop(0, 8, sum_b, 0, unroll=2)
    for d in order[:3]:
        fars.append(
            remote(quart_b.at[(x + d) % 4], far_b.at[d], f_send.at[1, d], f_recv.at[1, d],
                   device(seq, zh, (x + d) % 4, y, core))
        )
        fars[-1].start()
    outer_second(0)
    outer_second(1)
    outer_second(2)
    for copy in fars:
        chain(1)
        copy.wait_recv()

    def sum_far(p, _):
        one = quart_a[p, :, y].astype(F32)
        two = quart_b[x, p].astype(F32)
        for d in (1, 2, 3):
            one += far_a[d, p].astype(F32)
            two += far_b[d, p].astype(F32)
        for zt in range(2):
            for a, value in enumerate((one[zt], two[zt])):
                wide[zt, a, pl.ds(2 * p, 8, stride=16), :] = value[0:8]
                wide[zt, a, pl.ds(2 * p + 1, 8, stride=16), :] = value[8:16]
        return 0

    lax.fori_loop(0, 8, sum_far, 0, unroll=4)
    for zt in range(2):
        for a in range(2):
            back[zt, a] = wide[zt, a].astype(BF16).reshape(8, 16, 128)
    backs = []
    for k, (zt, px, pc) in enumerate(targets):
        backs.append(
            remote(back.at[zt, :, px * 2 + pc], rows.at[zh, :, me], b_send.at[k], b_recv.at[k],
                   device(seq, zt, px, y, pc))
        )
        backs[-1].start()
    rows[zh, :, me] = back[zh, :, me]
    outer_forward(0)
    chain(5)

    @pl.when(is_mid)
    def _():
        hidden_copy(far_end, 0, beside).wait_recv()
        hidden_copy(far_end, 4, beside).start()

    outer_forward(1)
    chain(2)
    for copy in backs:
        copy.wait_recv()
    outer_forward(2)
    chain(5)
    for k in range(3):
        chain(1)
        outer_finish(k)
    chain(CHUNKS + LAG)

    @pl.when(is_mid)
    def _():
        def step(k, _):
            mid_copy(k).wait_send()
            total_copy(k).wait_send()
            return 0

        lax.fori_loop(0, CHUNKS, step, 0)
        for k in range(5):
            hidden_copy(seq, k, beside).wait_send()

    @pl.when(is_end)
    def _():
        def step(k, _):
            end_copy(k).wait_send()
            total_copy(k).wait_recv()
            return 0

        lax.fori_loop(0, CHUNKS, step, 0)
        hidden_copy(seq, 0, beside).wait_send()
        for source in (near_end, mid, far_end):
            hidden_copy(source, 0, beside).wait_recv()

    for copy in outer_s:
        copy.wait_recv()
    own_rows.wait()
    for pair in swaps:
        for copy in pair:
            copy.wait_send()
    for copy in nears + fars + backs + outer_a + outer_b + outer_f + outer_s:
        copy.wait_send()


def reduce(slot_rows, slot_cols, count, sums, hidden, grad_pre, everything, outer_y, outer_x):
    vmem = pl.BlockSpec(memory_space=pltpu.VMEM)
    dma = pltpu.SemaphoreType.DMA
    slot = (SLOTS, 128, 128)
    return pl.pallas_call(
        reduce_kernel,
        out_shape=(
            jax.ShapeDtypeStruct((2, 2, 8, 16, 128), BF16),
            jax.ShapeDtypeStruct(slot, BF16),
            jax.ShapeDtypeStruct((4, COLS, 128, 128), BF16),
            jax.ShapeDtypeStruct((4, 4, 2, 8, 2, 4, 16, 128), BF16),
        ),
        in_specs=[pl.BlockSpec(memory_space=pltpu.SMEM)] * 3 + [vmem] * 7,
        out_specs=(vmem,) * 4,
        scratch_shapes=[
            pltpu.VMEM((2, 4, 2, 8, 2, 4, 16, 128), BF16),
            pltpu.VMEM(slot, BF16),
            pltpu.VMEM((4, 8, 2, 4, 16, 128), BF16),
            pltpu.VMEM((4, 4, 8, 2, 16, 128), BF16),
            pltpu.VMEM((4, 8, 2, 4, 16, 128), BF16),
            pltpu.VMEM((4, 4, 8, 2, 16, 128), BF16),
            pltpu.VMEM((4, 8, 2, 4, 16, 128), BF16),
            pltpu.VMEM((4, 4, 8, 2, 16, 128), BF16),
            pltpu.VMEM((8, 2, 4, 16, 128), BF16),
            pltpu.VMEM((4, 8, 2, 16, 128), BF16),
            pltpu.VMEM((4, 8, 2, 16, 128), BF16),
            pltpu.VMEM((4, 8, 2, 16, 128), BF16),
            pltpu.VMEM((2, 2, 128, 128), F32),
            pltpu.VMEM((2, 2, 8, 16, 128), BF16),
            pltpu.VMEM(slot, BF16),
            pltpu.VMEM(slot, BF16),
            pltpu.VMEM(slot, BF16),
            dma((2, 4)), dma((2, 4)), dma((2, 4)), dma((2, 4)), dma((2, 4)), dma((2, 4)),
            dma((15,)), dma((15,)),
            dma((CHUNKS,)), dma((CHUNKS,)), dma((CHUNKS,)), dma((CHUNKS,)),
            dma((CHUNKS,)), dma((CHUNKS,)),
            dma((5,)), dma((4,)), dma, dma((3, 2, 3)), dma((3, 2, 3)), dma((3, 2, 2)), dma((3, 2, 2)),
            dma((3, 2, 2)), dma((3, 2, 2)), dma((3, 2, 4)), dma((3, 2, 4)),
        ],
        compiler_params=pltpu.CompilerParams(
            collective_id=2, has_side_effects=True, vmem_limit_bytes=24 << 20
        ),
        cost_estimate=pl.CostEstimate(flops=0, bytes_accessed=64 << 20, transcendentals=0),
        name="reduce_sums",
    )(
        slot_rows, slot_cols, count, sums, hidden, grad_pre,
        everything, everything.reshape(2, 64, 128, 128), outer_y, outer_x,
    )


STEP = 36


def finish_kernel(
    row_hbm, col_hbm, count_ref, act_ref, gain_ref, grad_ref, sums_ref,
    hidden_ref, grads_ref, total_ref, layer_ref, gin_ref, in_ref, out_ref,
    turned, row_ref, col_ref, local_sem,
):
    first_col = lax.axis_index("hid") * COLS

    @pl.when(pl.program_id(0) == 0)
    def _():
        loads = [
            pltpu.make_async_copy(src, dst, local_sem.at[k])
            for k, (src, dst) in enumerate(
                ((row_hbm, row_ref), (col_hbm, col_ref))
            )
        ]
        for load in loads:
            load.start()
        for load in loads:
            load.wait()
        for c in range(COLS):
            for g in range(4):
                turned[c, :, g * 128 : (g + 1) * 128] = hidden_ref[g, c].T

    count = count_ref[0]
    for k in range(STEP):
        s = pl.program_id(0) * STEP + k
        row = row_ref[s]
        col = col_ref[s] - first_col
        rows = jnp.concatenate([grads_ref[g, row] for g in range(4)], axis=0)
        value = dot(turned[col], rows, ((1,), (0,)))
        out_ref[k] = jnp.where(s < count, value, 0.0)
        in_ref[k] = total_ref[s].astype(F32)

    @pl.when(pl.program_id(0) == 0)
    def _():
        sums = []
        for a in range(2):
            both = sums_ref[0, a].astype(F32) + sums_ref[1, a].astype(F32)
            sums.append(
                jnp.concatenate(
                    [both[p // 8, 2 * (p % 8) : 2 * (p % 8) + 2, :] for p in range(64)], axis=1
                )
            )
        x_hat, inv_std = layer_norm(act_ref)
        layer_ref[...] = (act_ref[...].astype(F32) + sums[0]).astype(BF16)
        scaled = sums[1] * gain_ref[...]
        mean_g = jnp.sum(scaled, axis=-1, keepdims=True) * (1.0 / WIDTH)
        mean_gx = jnp.sum(scaled * x_hat, axis=-1, keepdims=True) * (1.0 / WIDTH)
        gin_ref[...] = (
            inv_std * (scaled - mean_g - x_hat * mean_gx) + grad_ref[...].astype(F32)
        ).astype(BF16)


def finish(rows, cols, count, act, gain, grad, sums, hidden, grads, totals):
    vmem = pl.BlockSpec(memory_space=pltpu.VMEM)
    hbm = pl.BlockSpec(memory_space=pltpu.HBM)
    pin = functools.partial(pltpu.with_memory_space_constraint, memory_space=pltpu.HBM)
    block = pl.BlockSpec((STEP, 128, 128), lambda i: (i, 0, 0))
    line = pl.BlockSpec((2, WIDTH), lambda i: (0, 0))
    shape = jax.ShapeDtypeStruct((SLOTS, 128, 128), F32)
    narrow = jax.ShapeDtypeStruct((2, WIDTH), BF16)
    return pl.pallas_call(
        finish_kernel,
        grid=(SLOTS // STEP,),
        out_shape=(narrow, narrow, shape, shape),
        in_specs=[hbm] * 2 + [pl.BlockSpec(memory_space=pltpu.SMEM)] + [vmem] * 7,
        out_specs=(line, line, block, block),
        scratch_shapes=[
            pltpu.VMEM((COLS, 128, 512), BF16),
            pltpu.SMEM((SLOTS,), jnp.int32),
            pltpu.SMEM((SLOTS,), jnp.int32),
            pltpu.SemaphoreType.DMA((2,)),
        ],
        compiler_params=pltpu.CompilerParams(vmem_limit_bytes=8 << 20),
        name="block_gradients",
    )(pin(rows), pin(cols), count, act, gain, grad, sums, hidden, grads, totals)


def local(activations, ln_gain, in_blocks, out_blocks, block_row, block_col, block_count, grad_out):
    gain = ln_gain.reshape(1, WIDTH)
    everything, outer_y, outer_x = gather(activations, gain, grad_out)
    sums, hidden, grad_pre = compute(
        block_row, block_col, block_count, everything.reshape(2, 64, 128, 128), in_blocks, out_blocks
    )
    row_sums, totals, hiddens, grads = reduce(
        block_row, block_col, block_count, sums.reshape(2, 4, 2, 8, 2, 4, 16, 128), hidden, grad_pre,
        everything, outer_y, outer_x,
    )
    return finish(
        block_row, block_col, block_count, activations, gain, grad_out, row_sums,
        hiddens, grads.reshape(4, 64, 128, 128), totals,
    )


def solution(mesh):
    rows, blocks, slots = P(("seq", "hid"), None), P("hid", None, None), P("hid")
    in_specs = (rows, P(), blocks, blocks, slots, slots, slots, rows)
    out_specs = (rows, rows, blocks, blocks)
    return jax.shard_map(local, mesh=mesh, in_specs=in_specs, out_specs=out_specs, check_vma=False)
```

```python
import functools

import jax
import jax.numpy as jnp
from jax import lax
from jax.experimental import pallas as pl
from jax.experimental.pallas import tpu as pltpu
from jax.sharding import PartitionSpec as P

F32 = jnp.float32
BF16 = jnp.bfloat16
MESH = pl.DeviceIdType.MESH
WIDTH = 8192
SLOTS = 36
COLS = 3
CHUNK = 1
CHUNKS = SLOTS // CHUNK
LAG = 5


def place():
    seq, hid = lax.axis_index("seq"), lax.axis_index("hid")
    return seq, hid // 32, (hid // 8) % 4, (hid // 2) % 4, hid % 2


def device(seq, zh, x, y, core):
    return (seq, zh * 32 + x * 8 + y * 2 + core)


def remote(src, dst, send, recv, to):
    return pltpu.make_async_remote_copy(
        src_ref=src, dst_ref=dst, send_sem=send, recv_sem=recv, device_id=to, device_id_type=MESH
    )


def meet(peers):
    barrier = pltpu.get_barrier_semaphore()
    for peer in peers:
        pl.semaphore_signal(barrier, inc=1, device_id=peer, device_id_type=MESH)
    pl.semaphore_wait(barrier, len(peers))


def octet_peers(seq, zh, x, y, core):
    offsets = [(dx, dc) for dx in (2, 1, 3, 0) for dc in (0, 1) if (dx, dc) != (0, 0)]
    return [((x + dx) % 4, (core + dc) % 2) for dx, dc in offsets]


def layer_norm(act_ref):
    values = act_ref[...].astype(F32)
    mean = jnp.sum(values, axis=-1, keepdims=True) * (1.0 / WIDTH)
    centered = values - mean
    variance = jnp.sum(centered * centered, axis=-1, keepdims=True) * (1.0 / WIDTH)
    inv_std = lax.rsqrt(variance + 1e-05)
    return centered * inv_std, inv_std


def gather_kernel(
    act_hbm, gain_hbm, grad_hbm, all_ref, outer_y, outer_x,
    act_ref, gain_ref, grad_ref, wide, packed, landed,
    local_sem, a2a_send, a2a_recv, z_send, z_recv, s1_send, s1_recv,
    s2_send, s2_recv, fw_send, fw_recv, sw_send, sw_recv,
):
    seq, zh, x, y, core = place()
    me = x * 2 + core
    octet = octet_peers(seq, zh, x, y, core)
    xs = [(x + d) % 4 for d in (1, 3, 2)]
    ys = [(y + d) % 4 for d in (1, 3, 2)]
    planes = (zh, 1 - zh)
    sibling = device(seq, zh, x, y, 1 - core)
    loads = [
        pltpu.make_async_copy(src, dst, local_sem.at[k])
        for k, (src, dst) in enumerate(
            ((act_hbm, act_ref), (gain_hbm, gain_ref), (grad_hbm, grad_ref))
        )
    ]
    for load in loads:
        load.start()
    targets = [(0, px, pc) for px, pc in octet] + [(1, px, pc) for px, pc in octet]
    targets.append((1, x, core))
    peers = [device(seq, planes[f], px, y, pc) for f, px, pc in targets]
    peers += [device(seq, zh, x, py, core) for py in ys]
    peers += [device((seq + d) % 4, zh, x, y, core) for d in (1, 2, 3)]
    barrier = pltpu.get_barrier_semaphore()
    for peer in peers:
        pl.semaphore_signal(barrier, inc=1, device_id=peer, device_id_type=MESH)
    for load in loads:
        load.wait()
    x_hat, _ = layer_norm(act_ref)
    for a, rows in enumerate((x_hat * gain_ref[...], grad_ref[...].astype(F32))):
        for p in range(64):
            wide[a, 2 * p : 2 * p + 2, :] = rows[:, p * 128 : (p + 1) * 128]
        packed[a] = wide[a].astype(BF16).reshape(8, 16, 128)
    pl.semaphore_wait(barrier, len(peers))
    near, far = [], []
    for k in [*range(7, 15), *range(7)]:
        f, px, pc = targets[k]
        copy = remote(
            packed.at[:, px * 2 + pc], landed.at[zh, :, me], a2a_send.at[k], a2a_recv.at[k],
            peers[k],
        )
        copy.start()
        (far if f else near).append(copy)
    landed[zh, :, me] = packed[:, me]

    def relayout(zp):
        for a in range(2):
            wide[a] = landed[zp, a].astype(F32).reshape(128, 128)
            for p in range(8):
                first = wide[a, pl.ds(2 * p, 8, stride=16), :]
                second = wide[a, pl.ds(2 * p + 1, 8, stride=16), :]
                all_ref[a, x, core, p, zp, y] = jnp.concatenate([first, second], axis=0).astype(BF16)

    stage_ones, stage_twos, forwards, swaps, lines = {}, {}, {}, [], []

    def stage_one(f):
        zp = planes[f]
        for a in (0, 1):
            block = all_ref.at[a, x, core, :, zp, y]
            out = []
            for d in range(3):
                to = device(seq, zh, xs[d], y, core) if a == 0 else device(seq, zh, x, ys[d], core)
                out.append(remote(block, block, s1_send.at[f, a, d], s1_recv.at[f, a, d], to))
                out[-1].start()
            stage_ones[f, a] = out

    def piece(f, other, nx, ny):
        return outer_x.at[other, nx] if f else outer_y.at[other, :, ny]

    def along_z(f):
        zp = planes[f]
        for d in (1, 2, 3):
            lines.append(
                remote(all_ref.at[1, x, core, :, zp, y], piece(f, seq, x, y),
                       z_send.at[f, d - 1], z_recv.at[f, d - 1],
                       device((seq + d) % 4, zh, x, y, core))
            )
            lines[-1].start()

    def part(f, a, nx, ny, half):
        zp = planes[f]
        if a == 0:
            if half is None:
                return all_ref.at[0, :, core, :, zp, ny]
            return all_ref.at[0, pl.ds(2 * half, 2), core, :, zp, ny]
        if half is None:
            return all_ref.at[1, nx, core, :, zp]
        return all_ref.at[1, nx, core, pl.ds(4 * half, 4), zp]

    def ahead(a, d):
        if a == 0:
            return device(seq, zh, x, ys[d], core)
        return device(seq, zh, xs[d], y, core)

    def swap(f, a, k, block):
        copy = remote(block, block, sw_send.at[f, a, k], sw_recv.at[f, a, k], sibling)
        copy.start()
        swaps.append(copy)

    def stage_two(f):
        for a in (0, 1):
            for copy in stage_ones[f, a]:
                copy.wait_recv()
            for n in range(2):
                for d in range(2):
                    half = n if d == 0 else 1 - n
                    block = part(f, a, x, y, half)
                    stage_twos[f, a, d, half] = remote(
                        block, block, s2_send.at[f, a, d, half], s2_recv.at[f, a, d, half],
                        ahead(a, d),
                    )
                    stage_twos[f, a, d, half].start()
        for a in (0, 1):
            swap(f, a, 0, part(f, a, x, y, None))

    def forward(f):
        for a in (0, 1):
            out = []
            for d in range(2):
                stage_twos[f, a, d, d].wait_recv()
                block = part(f, a, xs[1 - d], ys[1 - d], d)
                out.append(
                    remote(block, block, fw_send.at[f, a, d], fw_recv.at[f, a, d], ahead(a, d))
                )
                out[-1].start()
            forwards[f, a] = out
        for a in (0, 1):
            for d in range(2):
                stage_twos[f, a, d, 1 - d].wait_recv()
                swap(f, a, 1 + d, part(f, a, xs[1 - d], ys[1 - d], None))

    def finish(f):
        for a in (0, 1):
            for copy in forwards[f, a]:
                copy.wait_recv()
            swap(f, a, 3, part(f, a, xs[2], ys[2], None))

    for copy in near:
        copy.wait_recv()
    relayout(zh)
    stage_one(0)
    for copy in far:
        copy.wait_recv()
    relayout(1 - zh)
    stage_one(1)
    stage_two(0)
    along_z(0)
    along_z(1)
    stage_two(1)
    forward(0)
    forward(1)
    finish(0)
    finish(1)
    for copy in swaps + lines:
        copy.wait_recv()
    for copy in near + far + lines + swaps:
        copy.wait_send()
    for copy in stage_twos.values():
        copy.wait_send()
    for group in (stage_ones, forwards):
        for copies in group.values():
            for copy in copies:
                copy.wait_send()


def gather(act, gain, grad):
    vmem = pl.BlockSpec(memory_space=pltpu.VMEM)
    hbm = pl.BlockSpec(memory_space=pltpu.HBM)
    dma = pltpu.SemaphoreType.DMA
    return pl.pallas_call(
        gather_kernel,
        out_shape=(
            jax.ShapeDtypeStruct((2, 4, 2, 8, 2, 4, 16, 128), BF16),
            jax.ShapeDtypeStruct((4, 8, 4, 16, 128), BF16),
            jax.ShapeDtypeStruct((4, 4, 8, 16, 128), BF16),
        ),
        in_specs=[hbm] * 3,
        out_specs=(vmem, vmem, vmem),
        scratch_shapes=[
            pltpu.VMEM((2, WIDTH), BF16),
            pltpu.VMEM((1, WIDTH), F32),
            pltpu.VMEM((2, WIDTH), BF16),
            pltpu.VMEM((2, 128, 128), F32),
            pltpu.VMEM((2, 8, 16, 128), BF16),
            pltpu.VMEM((2, 2, 8, 16, 128), BF16),
            dma((3,)), dma((15,)), dma((15,)), dma((2, 3)), dma((2, 3)),
            dma((2, 2, 3)), dma((2, 2, 3)), dma((2, 2, 2, 2)), dma((2, 2, 2, 2)),
            dma((2, 2, 2)), dma((2, 2, 2)), dma((2, 2, 4)), dma((2, 2, 4)),
        ],
        compiler_params=pltpu.CompilerParams(
            collective_id=1, has_side_effects=True, vmem_limit_bytes=12 << 20
        ),
        cost_estimate=pl.CostEstimate(flops=0, bytes_accessed=64 << 20, transcendentals=0),
        name="gather_rows",
    )(*(pltpu.with_memory_space_constraint(v, pltpu.HBM) for v in (act, gain, grad)))


def dot(a, b, dims):
    return lax.dot_general(a, b, (dims, ((), ())), preferred_element_type=F32)


GROUP = 36


def compute_kernel(
    row_hbm, col_hbm, count_ref, all_ref, in_hbm, out_hbm, total, hidden, grad_pre,
    row_ref, col_ref, in_ref, out_ref, pre, grad_hidden, local_sem,
):
    first_col = lax.axis_index("hid") * COLS
    loads = [
        pltpu.make_async_copy(src, dst, local_sem.at[k])
        for k, (src, dst) in enumerate(
            ((row_hbm, row_ref), (col_hbm, col_ref), (in_hbm, in_ref), (out_hbm, out_ref))
        )
    ]
    for load in loads:
        load.start()

    def clear(p, _):
        total[0, p] = jnp.zeros((128, 128), F32)
        total[1, p] = jnp.zeros((128, 128), F32)
        return 0

    lax.fori_loop(0, 64, clear, 0)
    pre[...] = jnp.zeros_like(pre)
    grad_hidden[...] = jnp.zeros_like(grad_hidden)
    for load in loads:
        load.wait()
    count = count_ref[0]

    def up(g, _):
        parts = []
        for k in range(GROUP):
            s = g * GROUP + k
            row = row_ref[s]
            live = s < count
            one = dot(all_ref[0, row], in_ref[s], ((1,), (0,)))
            two = dot(all_ref[1, row], out_ref[s], ((1,), (1,)))
            parts.append((s, jnp.where(live, one, 0.0), jnp.where(live, two, 0.0)))
        for s, one, two in parts:
            col = col_ref[s] - first_col
            pre[col] += one
            grad_hidden[col] += two
        return 0

    lax.fori_loop(0, SLOTS // GROUP, up, 0)
    for c in range(COLS):
        value = pre[c]
        sig = jax.nn.sigmoid(value)
        hidden[c] = (value * sig).astype(BF16)
        grad_pre[c] = (grad_hidden[c] * sig * (1.0 + value * (1.0 - sig))).astype(BF16)

    def down(g, _):
        parts = []
        for k in range(GROUP):
            s = g * GROUP + k
            row = row_ref[s]
            col = col_ref[s] - first_col
            live = s < count
            h, gp = hidden[col], grad_pre[col]
            one = dot(h, out_ref[s], ((1,), (0,)))
            two = dot(gp, in_ref[s], ((1,), (1,)))
            parts.append((s, row, jnp.where(live, one, 0.0), jnp.where(live, two, 0.0)))
        for s, row, one, two in parts:
            total[0, row] += one
            total[1, row] += two
        return 0

    lax.fori_loop(0, SLOTS // GROUP, down, 0)


def compute(rows, cols, count, everything, in_blocks, out_blocks):
    vmem = pl.BlockSpec(memory_space=pltpu.VMEM)
    hbm = pl.BlockSpec(memory_space=pltpu.HBM)
    pin = functools.partial(pltpu.with_memory_space_constraint, memory_space=pltpu.HBM)
    return pl.pallas_call(
        compute_kernel,
        out_shape=(
            jax.ShapeDtypeStruct((2, 64, 128, 128), F32),
            jax.ShapeDtypeStruct((COLS, 128, 128), BF16),
            jax.ShapeDtypeStruct((COLS, 128, 128), BF16),
        ),
        in_specs=[hbm] * 2 + [pl.BlockSpec(memory_space=pltpu.SMEM)] + [vmem] + [hbm] * 2,
        out_specs=(vmem, vmem, vmem),
        scratch_shapes=[
            pltpu.SMEM((SLOTS,), jnp.int32),
            pltpu.SMEM((SLOTS,), jnp.int32),
            pltpu.VMEM((SLOTS, 128, 128), BF16),
            pltpu.VMEM((SLOTS, 128, 128), BF16),
            pltpu.VMEM((COLS, 128, 128), F32),
            pltpu.VMEM((COLS, 128, 128), F32),
            pltpu.SemaphoreType.DMA((4,)),
        ],
        compiler_params=pltpu.CompilerParams(vmem_limit_bytes=24 << 20),
        name="block_products",
    )(pin(rows), pin(cols), count, everything, pin(in_blocks), pin(out_blocks))


def reduce_kernel(
    row_ref, col_ref, count_ref, wide_ref, hidden_ref, gp_ref, all_ref, blocks_ref, outer_y, outer_x,
    rows, total_ref, hiddens_ref, grads_ref, sums_ref, part_ref,
    swap_a, swap_b, half_a, half_b, near_a, near_b, quart_a, quart_b, far_a, far_b,
    wide, back,
    end_in, mid_own, mid_in,
    sw_send, sw_recv, n_send, n_recv, f_send, f_recv, b_send, b_recv,
    e_send, e_recv, m_send, m_recv, t_send, t_recv,
    h_send, h_recv, own_sem, oa_send, oa_recv, ob_send, ob_recv, of_send, of_recv, os_send, os_recv,
):
    seq, zh, x, y, core = place()
    me = x * 2 + core
    octet = octet_peers(seq, zh, x, y, core)
    sibling = device(seq, zh, x, y, 1 - core)
    beside = device(seq + 1 - 2 * (seq % 2), zh, x, y, core)
    across = device(3 - seq, zh, x, y, core)
    is_mid = jnp.logical_or(seq == 1, seq == 2)
    is_end = jnp.logical_or(seq == 0, seq == 3)
    targets = [(zh, px, pc) for px, pc in octet] + [(1 - zh, px, pc) for px, pc in octet]
    targets.append((1 - zh, x, core))
    peers = [device(seq, zt, px, y, pc) for zt, px, pc in targets]
    peers += [device(seq, zh, x, (y + d) % 4, core) for d in (1, 2, 3)]
    peers += [device((seq + d) % 4, zh, x, y, core) for d in (1, 2, 3)]
    barrier = pltpu.get_barrier_semaphore()
    for peer in peers:
        pl.semaphore_signal(barrier, inc=1, device_id=peer, device_id_type=MESH)
    others = [(seq + d) % 4 for d in (1, 2, 3)]
    xs = [(x + d) % 4 for d in (1, 3, 2)]
    ys = [(y + d) % 4 for d in (1, 3, 2)]

    own_rows = pltpu.make_async_copy(all_ref.at[1], grads_ref.at[seq], own_sem)
    own_rows.start()

    def narrow(v, _):
        for c in range(2):
            for p in range(8):
                sums_ref[0, v, c, p] = wide_ref[0, v, c, p].astype(BF16)
                sums_ref[1, v, c, p] = wide_ref[1, v, c, p].astype(BF16)
        return 0

    lax.fori_loop(0, 4, narrow, 0)
    first_col = lax.axis_index("hid") * COLS
    count = count_ref[0]

    def product(g, _):
        for k in range(12):
            s = g * 12 + k
            row = jnp.clip(row_ref[s], 0, 63)
            col = jnp.clip(col_ref[s] - first_col, 0, COLS - 1)
            value = dot(blocks_ref[0, row], gp_ref[col], ((0,), (0,)))
            part_ref[s] = jnp.where(s < count, value, 0.0).astype(BF16)
        return 0

    lax.fori_loop(0, SLOTS // 12, product, 0)
    hiddens_ref[seq] = hidden_ref[...]
    for other in others:
        for n in range(8):
            grads_ref[other, x, core, n, zh, y] = outer_y[other, n, y]
            grads_ref[other, x, core, n, 1 - zh, y] = outer_x[other, x, n]
    pl.semaphore_wait(barrier, len(peers))

    def chunk(ref, k):
        return ref.at[pl.ds(k * CHUNK, CHUNK)]

    def end_copy(k):
        return remote(chunk(part_ref, k), chunk(end_in, k), e_send.at[k], e_recv.at[k], beside)

    def mid_copy(k):
        return remote(chunk(mid_own, k), chunk(mid_in, k), m_send.at[k], m_recv.at[k], across)

    def total_copy(k):
        return remote(chunk(total_ref, k), chunk(total_ref, k), t_send.at[k], t_recv.at[k], beside)

    def mid_first(k):
        end_copy(k).wait_recv()
        for j in range(CHUNK):
            s = k * CHUNK + j
            mid_own[s] = (end_in[s].astype(F32) + part_ref[s].astype(F32)).astype(BF16)
        mid_copy(k).start()

    def mid_second(k):
        mid_copy(k).wait_recv()
        for j in range(CHUNK):
            s = k * CHUNK + j
            total_ref[s] = (mid_own[s].astype(F32) + mid_in[s].astype(F32)).astype(BF16)
        total_copy(k).start()

    done = [0]

    def chain(steps):
        start, stop = done[0], min(done[0] + steps, CHUNKS + LAG)
        done[0] = stop

        @pl.when(is_mid)
        def _():
            def step(k, _):
                @pl.when(k < CHUNKS)
                def _():
                    mid_first(k)

                @pl.when(k >= LAG)
                def _():
                    mid_second(k - LAG)

                return 0

            lax.fori_loop(start, stop, step, 0)

    order = (2, 1, 3, 0)
    swaps = []
    for d in order:
        pair = (
            remote(sums_ref.at[0, (x + d) % 4, 1 - core], swap_a.at[d],
                   sw_send.at[0, d], sw_recv.at[0, d], sibling),
            remote(sums_ref.at[1, :, 1 - core, :, :, (y + d) % 4], swap_b.at[d],
                   sw_send.at[1, d], sw_recv.at[1, d], sibling),
        )
        for copy in pair:
            copy.start()
        swaps.append(pair)

    near_end = seq + 1 - 2 * (seq % 2)
    mid = 3 - seq
    far_end = mid + 1 - 2 * (mid % 2)

    def hidden_copy(source, k, to):
        block = hiddens_ref.at[source]
        return remote(block, block, h_send.at[k], h_recv.at[source], to)

    outer_a, outer_b, outer_f, outer_s = [], [], [], []
    planes = (zh, 1 - zh)
    def outer_block(other, f, nx, ny, half):
        if f:
            if half is None:
                return grads_ref.at[other, :, core, :, planes[1], ny]
            return grads_ref.at[other, pl.ds(2 * half, 2), core, :, planes[1], ny]
        if half is None:
            return grads_ref.at[other, nx, core, :, planes[0]]
        return grads_ref.at[other, nx, core, pl.ds(4 * half, 4), planes[0]]

    def outer_to(f, d):
        return device(seq, zh, x, ys[d], core) if f else device(seq, zh, xs[d], y, core)

    def outer_swap(k, f, n, block):
        copy = remote(block, block, os_send.at[k, f, n], os_recv.at[k, f, n], sibling)
        copy.start()
        outer_s.append(copy)

    def outer_first(k):
        other = others[k]
        for f in range(2):
            block = outer_x.at[other, x] if f else outer_y.at[other, :, y]
            place_there = grads_ref.at[other, x, core, :, planes[f], y]
            for d in range(3):
                to = device(seq, zh, xs[d], y, core) if f else device(seq, zh, x, ys[d], core)
                outer_a.append(
                    remote(block, place_there, oa_send.at[k, f, d], oa_recv.at[k, f, d], to)
                )
                outer_a[-1].start()

    def outer_second(k):
        other = others[k]
        for copy in outer_a[6 * k : 6 * k + 6]:
            copy.wait_recv()
        for f in range(2):
            block = outer_block(other, f, x, y, None)
            for d in range(2):
                outer_b.append(
                    remote(block, block, ob_send.at[k, f, d], ob_recv.at[k, f, d], outer_to(f, d))
                )
                outer_b[-1].start()
        for f in range(2):
            outer_swap(k, f, 0, outer_block(other, f, x, y, None))

    def outer_forward(k):
        other = others[k]
        for f in range(2):
            for d in range(2):
                outer_b[4 * k + 2 * f + d].wait_recv()
                block = outer_block(other, f, xs[1 - d], ys[1 - d], d)
                outer_f.append(
                    remote(block, block, of_send.at[k, f, d], of_recv.at[k, f, d], outer_to(f, d))
                )
                outer_f[-1].start()
            for d in range(2):
                outer_swap(k, f, 1 + d, outer_block(other, f, xs[1 - d], ys[1 - d], None))

    def outer_finish(k):
        other = others[k]
        for f in range(2):
            for d in range(2):
                outer_f[4 * k + 2 * f + d].wait_recv()
            outer_swap(k, f, 3, outer_block(other, f, xs[2], ys[2], None))

    @pl.when(is_end)
    def _():
        def step(k, _):
            end_copy(k).start()
            return 0

        lax.fori_loop(0, 12, step, 0)
        hidden_copy(seq, 0, beside).start()
        lax.fori_loop(12, CHUNKS, step, 0)

    @pl.when(is_mid)
    def _():
        hidden_copy(seq, 0, beside).start()
        hidden_copy(seq, 1, across).start()

    nears = []
    for d, (copy_a, copy_b) in zip(order[:3], swaps):
        copy_a.wait_recv()

        def add_a(p, _):
            half_a[d, p] = (
                sums_ref[0, (x + d) % 4, core, p].astype(F32) + swap_a[d, p].astype(F32)
            ).astype(BF16)
            return 0

        lax.fori_loop(0, 8, add_a, 0, unroll=4)
        nears.append(
            remote(half_a.at[d], near_a.at[d], n_send.at[0, d], n_recv.at[0, d],
                   device(seq, zh, (x + d) % 4, y, core))
        )
        nears[-1].start()
        copy_b.wait_recv()

        def add_b(p, _):
            for v in range(4):
                half_b[d, v, p] = (
                    sums_ref[1, v, core, p, :, (y + d) % 4].astype(F32)
                    + swap_b[d, v, p].astype(F32)
                ).astype(BF16)
            return 0

        lax.fori_loop(0, 8, add_b, 0, unroll=2)
        nears.append(
            remote(half_b.at[d], near_b.at[d], n_send.at[1, d], n_recv.at[1, d],
                   device(seq, zh, x, (y + d) % 4, core))
        )
        nears[-1].start()
        chain(2)
    for k in range(3):
        outer_first(k)
    for copy in swaps[3]:
        copy.wait_recv()
    for copy in nears[0::2]:
        chain(5)
        copy.wait_recv()

    @pl.when(is_mid)
    def _():
        hidden_copy(near_end, 0, beside).wait_recv()
        hidden_copy(near_end, 2, across).start()
        hidden_copy(mid, 0, beside).wait_recv()
        hidden_copy(mid, 3, beside).start()


    def sum_a(p, _):
        value = sums_ref[0, x, core, p].astype(F32) + swap_a[0, p].astype(F32)
        for d in (1, 2, 3):
            value += near_a[d, p].astype(F32)
        quart_a[p] = value.astype(BF16)
        return 0

    lax.fori_loop(0, 8, sum_a, 0, unroll=4)
    fars = []
    for d in order[:3]:
        fars.append(
            remote(quart_a.at[:, :, (y + d) % 4], far_a.at[d], f_send.at[0, d], f_recv.at[0, d],
                   device(seq, zh, x, (y + d) % 4, core))
        )
        fars[-1].start()

    for copy in nears[1::2]:
        chain(1)
        copy.wait_recv()

    def sum_b(p, _):
        for v in range(4):
            value = sums_ref[1, v, core, p, :, y].astype(F32) + swap_b[0, v, p].astype(F32)
            for d in (1, 2, 3):
                value += near_b[d, v, p].astype(F32)
            quart_b[v, p] = value.astype(BF16)
        return 0

    lax.fori_loop(0, 8, sum_b, 0, unroll=2)
    for d in order[:3]:
        fars.append(
            remote(quart_b.at[(x + d) % 4], far_b.at[d], f_send.at[1, d], f_recv.at[1, d],
                   device(seq, zh, (x + d) % 4, y, core))
        )
        fars[-1].start()
    outer_second(0)
    outer_second(1)
    outer_second(2)
    for copy in fars:
        chain(1)
        copy.wait_recv()

    def sum_far(p, _):
        one = quart_a[p, :, y].astype(F32)
        two = quart_b[x, p].astype(F32)
        for d in (1, 2, 3):
            one += far_a[d, p].astype(F32)
            two += far_b[d, p].astype(F32)
        for zt in range(2):
            for a, value in enumerate((one[zt], two[zt])):
                wide[zt, a, pl.ds(2 * p, 8, stride=16), :] = value[0:8]
                wide[zt, a, pl.ds(2 * p + 1, 8, stride=16), :] = value[8:16]
        return 0

    lax.fori_loop(0, 8, sum_far, 0, unroll=4)
    for zt in range(2):
        for a in range(2):
            back[zt, a] = wide[zt, a].astype(BF16).reshape(8, 16, 128)
    backs = []
    for k, (zt, px, pc) in enumerate(targets):
        backs.append(
            remote(back.at[zt, :, px * 2 + pc], rows.at[zh, :, me], b_send.at[k], b_recv.at[k],
                   device(seq, zt, px, y, pc))
        )
        backs[-1].start()
    rows[zh, :, me] = back[zh, :, me]
    outer_forward(0)
    chain(5)

    @pl.when(is_mid)
    def _():
        hidden_copy(far_end, 0, beside).wait_recv()
        hidden_copy(far_end, 4, beside).start()

    outer_forward(1)
    chain(2)
    for copy in backs:
        copy.wait_recv()
    outer_forward(2)
    chain(5)
    for k in range(3):
        chain(1)
        outer_finish(k)
    chain(CHUNKS + LAG)

    @pl.when(is_mid)
    def _():
        def step(k, _):
            mid_copy(k).wait_send()
            total_copy(k).wait_send()
            return 0

        lax.fori_loop(0, CHUNKS, step, 0)
        for k in range(5):
            hidden_copy(seq, k, beside).wait_send()

    @pl.when(is_end)
    def _():
        def step(k, _):
            end_copy(k).wait_send()
            total_copy(k).wait_recv()
            return 0

        lax.fori_loop(0, CHUNKS, step, 0)
        hidden_copy(seq, 0, beside).wait_send()
        for source in (near_end, mid, far_end):
            hidden_copy(source, 0, beside).wait_recv()

    for copy in outer_s:
        copy.wait_recv()
    own_rows.wait()
    for pair in swaps:
        for copy in pair:
            copy.wait_send()
    for copy in nears + fars + backs + outer_a + outer_b + outer_f + outer_s:
        copy.wait_send()


def reduce(slot_rows, slot_cols, count, sums, hidden, grad_pre, everything, outer_y, outer_x):
    vmem = pl.BlockSpec(memory_space=pltpu.VMEM)
    dma = pltpu.SemaphoreType.DMA
    slot = (SLOTS, 128, 128)
    return pl.pallas_call(
        reduce_kernel,
        out_shape=(
            jax.ShapeDtypeStruct((2, 2, 8, 16, 128), BF16),
            jax.ShapeDtypeStruct(slot, BF16),
            jax.ShapeDtypeStruct((4, COLS, 128, 128), BF16),
            jax.ShapeDtypeStruct((4, 4, 2, 8, 2, 4, 16, 128), BF16),
        ),
        in_specs=[pl.BlockSpec(memory_space=pltpu.SMEM)] * 3 + [vmem] * 7,
        out_specs=(vmem,) * 4,
        scratch_shapes=[
            pltpu.VMEM((2, 4, 2, 8, 2, 4, 16, 128), BF16),
            pltpu.VMEM(slot, BF16),
            pltpu.VMEM((4, 8, 2, 4, 16, 128), BF16),
            pltpu.VMEM((4, 4, 8, 2, 16, 128), BF16),
            pltpu.VMEM((4, 8, 2, 4, 16, 128), BF16),
            pltpu.VMEM((4, 4, 8, 2, 16, 128), BF16),
            pltpu.VMEM((4, 8, 2, 4, 16, 128), BF16),
            pltpu.VMEM((4, 4, 8, 2, 16, 128), BF16),
            pltpu.VMEM((8, 2, 4, 16, 128), BF16),
            pltpu.VMEM((4, 8, 2, 16, 128), BF16),
            pltpu.VMEM((4, 8, 2, 16, 128), BF16),
            pltpu.VMEM((4, 8, 2, 16, 128), BF16),
            pltpu.VMEM((2, 2, 128, 128), F32),
            pltpu.VMEM((2, 2, 8, 16, 128), BF16),
            pltpu.VMEM(slot, BF16),
            pltpu.VMEM(slot, BF16),
            pltpu.VMEM(slot, BF16),
            dma((2, 4)), dma((2, 4)), dma((2, 4)), dma((2, 4)), dma((2, 4)), dma((2, 4)),
            dma((15,)), dma((15,)),
            dma((CHUNKS,)), dma((CHUNKS,)), dma((CHUNKS,)), dma((CHUNKS,)),
            dma((CHUNKS,)), dma((CHUNKS,)),
            dma((5,)), dma((4,)), dma, dma((3, 2, 3)), dma((3, 2, 3)), dma((3, 2, 2)), dma((3, 2, 2)),
            dma((3, 2, 2)), dma((3, 2, 2)), dma((3, 2, 4)), dma((3, 2, 4)),
        ],
        compiler_params=pltpu.CompilerParams(
            collective_id=2, has_side_effects=True, vmem_limit_bytes=24 << 20
        ),
        cost_estimate=pl.CostEstimate(flops=0, bytes_accessed=64 << 20, transcendentals=0),
        name="reduce_sums",
    )(
        slot_rows, slot_cols, count, sums, hidden, grad_pre,
        everything, everything.reshape(2, 64, 128, 128), outer_y, outer_x,
    )


PIECE = 6


def finish_kernel(
    row_hbm, col_hbm, count_ref, act_ref, gain_ref, grad_ref, sums_ref,
    hidden_ref, grads_ref, total_ref, layer_ref, gin_ref, in_ref, out_ref,
    turned, row_ref, col_ref, local_sem, wide_in, wide_out, in_sem, out_sem,
):
    first_col = lax.axis_index("hid") * COLS

    loads = [
        pltpu.make_async_copy(src, dst, local_sem.at[k])
        for k, (src, dst) in enumerate(((row_hbm, row_ref), (col_hbm, col_ref)))
    ]
    for load in loads:
        load.start()
    stores = []

    def store(k, wide, hbm, sem):
        part = pl.ds(k * PIECE, PIECE)
        stores.append(pltpu.make_async_copy(wide.at[part], hbm.at[part], sem.at[k]))
        stores[-1].start()

    for s in range(SLOTS):
        wide_in[s] = total_ref[s].astype(F32)
        if s % PIECE == PIECE - 1:
            store(s // PIECE, wide_in, in_ref, in_sem)
    for c in range(COLS):
        for g in range(4):
            turned[c, :, g * 128 : (g + 1) * 128] = hidden_ref[g, c].T
    for load in loads:
        load.wait()
    count = count_ref[0]
    for s in range(SLOTS):
        row = row_ref[s]
        col = col_ref[s] - first_col
        rows = jnp.concatenate([grads_ref[g, row] for g in range(4)], axis=0)
        value = dot(turned[col], rows, ((1,), (0,)))
        wide_out[s] = jnp.where(s < count, value, 0.0)
        if s % PIECE == PIECE - 1:
            store(s // PIECE, wide_out, out_ref, out_sem)
    sums = []
    for a in range(2):
        both = sums_ref[0, a].astype(F32) + sums_ref[1, a].astype(F32)
        sums.append(
            jnp.concatenate(
                [both[p // 8, 2 * (p % 8) : 2 * (p % 8) + 2, :] for p in range(64)], axis=1
            )
        )
    x_hat, inv_std = layer_norm(act_ref)
    layer_ref[...] = (act_ref[...].astype(F32) + sums[0]).astype(BF16)
    scaled = sums[1] * gain_ref[...]
    mean_g = jnp.sum(scaled, axis=-1, keepdims=True) * (1.0 / WIDTH)
    mean_gx = jnp.sum(scaled * x_hat, axis=-1, keepdims=True) * (1.0 / WIDTH)
    gin_ref[...] = (
        inv_std * (scaled - mean_g - x_hat * mean_gx) + grad_ref[...].astype(F32)
    ).astype(BF16)
    for copy in stores:
        copy.wait()


def finish(rows, cols, count, act, gain, grad, sums, hidden, grads, totals):
    vmem = pl.BlockSpec(memory_space=pltpu.VMEM)
    hbm = pl.BlockSpec(memory_space=pltpu.HBM)
    pin = functools.partial(pltpu.with_memory_space_constraint, memory_space=pltpu.HBM)
    shape = jax.ShapeDtypeStruct((SLOTS, 128, 128), F32)
    narrow = jax.ShapeDtypeStruct((2, WIDTH), BF16)
    return pl.pallas_call(
        finish_kernel,
        out_shape=(narrow, narrow, shape, shape),
        in_specs=[hbm] * 2 + [pl.BlockSpec(memory_space=pltpu.SMEM)] + [vmem] * 7,
        out_specs=(vmem, vmem, hbm, hbm),
        scratch_shapes=[
            pltpu.VMEM((COLS, 128, 512), BF16),
            pltpu.SMEM((SLOTS,), jnp.int32),
            pltpu.SMEM((SLOTS,), jnp.int32),
            pltpu.SemaphoreType.DMA((2,)),
            pltpu.VMEM((SLOTS, 128, 128), F32),
            pltpu.VMEM((SLOTS, 128, 128), F32),
            pltpu.SemaphoreType.DMA((SLOTS // PIECE,)),
            pltpu.SemaphoreType.DMA((SLOTS // PIECE,)),
        ],
        compiler_params=pltpu.CompilerParams(vmem_limit_bytes=8 << 20),
        name="block_gradients",
    )(pin(rows), pin(cols), count, act, gain, grad, sums, hidden, grads, totals)


def local(activations, ln_gain, in_blocks, out_blocks, block_row, block_col, block_count, grad_out):
    gain = ln_gain.reshape(1, WIDTH)
    everything, outer_y, outer_x = gather(activations, gain, grad_out)
    sums, hidden, grad_pre = compute(
        block_row, block_col, block_count, everything.reshape(2, 64, 128, 128), in_blocks, out_blocks
    )
    row_sums, totals, hiddens, grads = reduce(
        block_row, block_col, block_count, sums.reshape(2, 4, 2, 8, 2, 4, 16, 128), hidden, grad_pre,
        everything, outer_y, outer_x,
    )
    return finish(
        block_row, block_col, block_count, activations, gain, grad_out, row_sums,
        hiddens, grads.reshape(4, 64, 128, 128), totals,
    )


def solution(mesh):
    rows, blocks, slots = P(("seq", "hid"), None), P("hid", None, None), P("hid")
    in_specs = (rows, P(), blocks, blocks, slots, slots, slots, rows)
    out_specs = (rows, rows, blocks, blocks)
    return jax.shard_map(local, mesh=mesh, in_specs=in_specs, out_specs=out_specs, check_vma=False)
```
